128 devices in a mesh: src: 16 (over x, z), tgt: 8 (over y, core).
Axes of the slice: x: 4, y: 4, z: 4, core: 2. Of those that a mesh axis runs over, the one named last changes fastest.
Arguments:
- source_embed: bfloat16 [32, 131072], P('tgt', 'src'), may hold values from -4 to 4
- target_embed: bfloat16 [32, 131072], P('src', 'tgt'), may hold values from -4 to 4
- target_potential: float32 [131072], P('tgt'), may hold values from -15 to 15
- log_source_mass: float32 [131072], P('src'), may hold values from -14 to -10
- log_target_mass: float32 [131072], P('tgt'), may hold values from -14 to -10
- tile_list: int32 [16, 8, 2, 64], P('src', 'tgt'), may hold values from 0 to 31, as said below
- counts: int32 [16, 8], P('src', 'tgt'), may hold values from 8 to 64, as said below
Outputs:
- row_potential: float32 [131072], P('src')
- column_potential: float32 [131072], P('tgt')
The draws below stay inside these ranges and needn't reach their ends.
Inputs may be any that keep to these rules, and one draw needn't show every extreme that they name: `tile_list`: on device (s, t) the first counts[s, t] entries are distinct pairs; every source tile and every target tile lies in some live pair; entries past the count are valid tile numbers but not live. `counts`: some device's count is 64 in every draw.
All inputs are finite; a program needn't handle non-finite values.
Results may differ from the reference program's by a relative error of at most 0.0029.
Values may be sent and summed in bfloat16 or wider, within the bound.
No kernel may reach another device: no remote copies, remote signals or barrier semaphores. Data moves between devices by JAX's collectives and lax.ppermute only.
A program may use at most 64 MiB of HBM per device.

```python
import jax
import jax.numpy as jnp
from jax import lax

TILE = 512
E = 32
S_TILES = 16
T_TILES = 32
CAP = 64
N_CELLS = 131072
M_CELLS = 131072
N_SRC = 16
N_TGT = 8


def deal_tiles(key):
    pairs = S_TILES * T_TILES
    row_share = S_TILES // N_TGT
    col_share = T_TILES // N_SRC
    forced = max(row_share, col_share)
    pair_index = jnp.arange(pairs, dtype=jnp.int32)
    row_of = pair_index // T_TILES
    col_of = pair_index % T_TILES
    src_dev = jnp.arange(N_SRC, dtype=jnp.int32)[:, None, None]
    tgt_dev = jnp.arange(N_TGT, dtype=jnp.int32)[None, :, None]
    row_rank = row_of // N_TGT
    col_rank = col_of // N_SRC
    matched = row_rank % col_share == col_rank if row_share >= col_share else col_rank % row_share == row_rank
    needed = ((row_of % N_TGT)[None, None, :] == tgt_dev) & ((col_of % N_SRC)[None, None, :] == src_dev) & matched[None, None, :]
    jitter = jax.random.randint(jax.random.fold_in(key, 11), (N_SRC, N_TGT, pairs), 0, 1 << 16)
    ranking = jnp.where(needed, 0, jitter + 1) * pairs + pair_index[None, None, :]
    chosen = jnp.argsort(ranking, axis=-1)[..., :CAP].astype(jnp.int32)
    tile_list = jnp.stack((chosen // T_TILES, chosen % T_TILES), axis=2).astype(jnp.int32)
    spread = jax.random.randint(jax.random.fold_in(key, 12), (N_SRC, N_TGT), 0, CAP + 1)
    counts = jnp.maximum(spread * spread // CAP, max(forced, CAP // 8))
    busiest = jax.random.randint(jax.random.fold_in(key, 13), (), 0, N_SRC * N_TGT)
    device_number = jnp.arange(N_SRC * N_TGT, dtype=jnp.int32).reshape(N_SRC, N_TGT)
    counts = jnp.where(device_number == busiest, CAP, counts)
    return (tile_list, counts.astype(jnp.int32))


def draw_tile_list(key, part):
    tile_list, counts = deal_tiles(key)
    return tile_list


def draw_counts(key, part):
    tile_list, counts = deal_tiles(key)
    return counts


def draw_target_potential(key, part):
    key = jax.random.fold_in(key, 21)
    values = jax.random.normal(jax.random.fold_in(key, 3), (M_CELLS,), jnp.float32)
    return (0.3 * jnp.clip(values, -6.0, 6.0)).astype(jnp.float32)


def level_of(own_key, dims, cuts, smallest, high):
    def one(axis_at, parts):
        draws = jax.random.uniform(jax.random.fold_in(jax.random.fold_in(own_key, 6), axis_at), (parts,), jnp.float32, smallest / len(cuts), high / len(cuts))
        return jnp.repeat(jnp.exp(draws), dims[axis_at] // parts).reshape((-1,) + (1,) * (len(dims) - axis_at - 1))

    gain = one(*cuts[0])
    for cut in cuts[1:]:
        gain = gain * one(*cut)
    return gain


def scatter_about(stream_key, dims, width, bound, pieces=(), kind=jnp.bfloat16):
    entries = jax.random.normal(stream_key, dims, jnp.float32) * width
    if len(pieces) > 0:
        entries = level_of(stream_key, dims, pieces, -0.22, 0.18) * entries
    return jnp.clip(entries, min=-bound, max=bound).astype(kind)


def setup_inputs(seed: int = 0) -> dict:
    key_of = jax.random.split(jax.random.key(seed), 8)
    source_embed = scatter_about(key_of[0], (E, N_CELLS), 0.7, 4.0, ((0, 8), (1, 16)))
    target_embed = scatter_about(key_of[1], (E, M_CELLS), 0.7, 4.0, ((0, 16), (1, 8)))
    target_potential = draw_target_potential(jax.random.fold_in(key_of[7], 71), 0)
    log_source_mass = jnp.clip(-14.0 + 4.0 * jax.random.uniform(key_of[3], (N_CELLS,), jnp.float32) ** level_of(key_of[3], (N_CELLS,), ((0, 16),), -0.2, 0.2), -14.0, -10.0)
    log_target_mass = jnp.clip(-14.0 + 4.0 * jax.random.uniform(key_of[4], (M_CELLS,), jnp.float32) ** level_of(key_of[4], (M_CELLS,), ((0, 8),), -0.2, 0.2), -14.0, -10.0)
    tile_list = draw_tile_list(jax.random.fold_in(key_of[7], 71), 0)
    counts = draw_counts(jax.random.fold_in(key_of[7], 71), 0)
    return {"source_embed": source_embed, "target_embed": target_embed, "target_potential": target_potential, "log_source_mass": log_source_mass, "log_target_mass": log_target_mass, "tile_list": tile_list, "counts": counts}


epsilon = 0.1
lowest = -1.0e30


def merge_pair(former, latter):
    highest = jnp.maximum(former[0], latter[0])
    return highest, former[1] * jnp.exp(former[0] - highest) + latter[1] * jnp.exp(latter[0] - highest)


def tile_cost(source_tile, target_tile):
    source_square = jnp.sum(jnp.square(source_tile.astype(jnp.float32)), axis=0)
    target_square = jnp.sum(jnp.square(target_tile.astype(jnp.float32)), axis=0)
    inner = jnp.dot(source_tile.T, target_tile, preferred_element_type=jnp.float32)
    return (source_square[:, None] + target_square[None, :] - 2.0 * inner) / (2.0 * E)


def reference(source_embed, target_embed, target_potential, log_source_mass, log_target_mass, tile_list, counts):
    source_base = jnp.arange(N_SRC, dtype=jnp.int32)[:, None, None] * S_TILES
    target_base = jnp.arange(N_TGT, dtype=jnp.int32)[None, :, None] * T_TILES
    source_index = (tile_list[:, :, 0, :] + source_base).reshape(-1).astype(jnp.int32)
    target_index = (tile_list[:, :, 1, :] + target_base).reshape(-1).astype(jnp.int32)
    alive_flags = (jnp.arange(CAP, dtype=jnp.int32)[None, None, :] < counts[:, :, None]).reshape(-1)

    def fetch_cost(source_at, target_at):
        source_tile = lax.dynamic_slice_in_dim(source_embed, source_at * TILE, TILE, 1)
        target_tile = lax.dynamic_slice_in_dim(target_embed, target_at * TILE, TILE, 1)
        return tile_cost(source_tile, target_tile)

    def row_step(state_pair, element):
        source_at, target_at, alive = element

        def update(totals):
            cost_tile = fetch_cost(source_at, target_at)
            pot_tile = lax.dynamic_slice_in_dim(target_potential, target_at * TILE, TILE)
            scores = (pot_tile[None, :] - cost_tile) / epsilon
            tile_max = jnp.max(scores, axis=1)
            tile_sum = jnp.sum(jnp.exp(scores - tile_max[:, None]), axis=1)
            offset = source_at * TILE
            previous = (lax.dynamic_slice_in_dim(totals[0], offset, TILE), lax.dynamic_slice_in_dim(totals[1], offset, TILE))
            updated = merge_pair(previous, (tile_max, tile_sum))
            return (lax.dynamic_update_slice_in_dim(totals[0], updated[0], offset, 0),
                    lax.dynamic_update_slice_in_dim(totals[1], updated[1], offset, 0))

        return lax.cond(alive, update, lambda totals: totals, state_pair), None

    row_init = (jnp.full((N_CELLS,), lowest, jnp.float32), jnp.zeros((N_CELLS,), jnp.float32))
    (row_max, row_sum), _ = lax.scan(row_step, row_init, (source_index, target_index, alive_flags))
    row_potential = epsilon * log_source_mass - epsilon * (row_max + jnp.log(row_sum))

    def col_step(state_pair, element):
        source_at, target_at, alive = element

        def update(totals):
            cost_tile = fetch_cost(source_at, target_at)
            pot_tile = lax.dynamic_slice_in_dim(row_potential, source_at * TILE, TILE)
            scores = (pot_tile[:, None] - cost_tile) / epsilon
            tile_max = jnp.max(scores, axis=0)
            tile_sum = jnp.sum(jnp.exp(scores - tile_max[None, :]), axis=0)
            offset = target_at * TILE
            previous = (lax.dynamic_slice_in_dim(totals[0], offset, TILE), lax.dynamic_slice_in_dim(totals[1], offset, TILE))
            updated = merge_pair(previous, (tile_max, tile_sum))
            return (lax.dynamic_update_slice_in_dim(totals[0], updated[0], offset, 0),
                    lax.dynamic_update_slice_in_dim(totals[1], updated[1], offset, 0))

        return lax.cond(alive, update, lambda totals: totals, state_pair), None

    col_init = (jnp.full((M_CELLS,), lowest, jnp.float32), jnp.zeros((M_CELLS,), jnp.float32))
    (col_max, col_sum), _ = lax.scan(col_step, col_init, (source_index, target_index, alive_flags))
    column_potential = epsilon * log_target_mass - epsilon * (col_max + jnp.log(col_sum))
    return row_potential, column_potential
```

```python
import functools

import jax
import jax.numpy as jnp
from jax import lax
from jax.experimental import pallas as pl
from jax.experimental.pallas import tpu as pltpu
from jax.sharding import PartitionSpec as P

TILE = 512
WIDTH = 32
DEPTH = 48
EPSILON = 0.1
HALF = float(WIDTH)
UNIT = 1.0 / (EPSILON * HALF)
ALPHA = UNIT * 1.4426950408889634
LOWEST = -1e30


def scaled_exp(value):
    return jnp.exp2(value * ALPHA)


def lse_kernel(red_row, keep_row, list_ref, count_ref, red_ref, keep_ref, bias_ref, out_ref, red_rows, keep_cols, top, total):
    red_tiles = red_ref.shape[1] // TILE
    keep_tiles = keep_ref.shape[1] // TILE

    def at_tile(tile):
        return pl.ds(pl.multiple_of(tile * TILE, TILE), TILE)

    def prepare_reduced(tile, _):
        at = at_tile(tile)
        cells = red_ref[:, at].astype(jnp.float32)
        bias = HALF * bias_ref[:, at] - 0.5 * jnp.sum(cells * cells, axis=0, keepdims=True)
        first = bias.astype(jnp.bfloat16).astype(jnp.float32)
        rest = bias - first
        second = rest.astype(jnp.bfloat16).astype(jnp.float32)
        filler = jnp.zeros((128 - WIDTH - 3, TILE), jnp.float32)
        rows = jnp.concatenate([cells, first, second, rest - second, filler], axis=0)
        red_rows[at, :] = jnp.transpose(rows).astype(jnp.bfloat16)
        return 0

    def prepare_kept(tile, _):
        at = at_tile(tile)
        keep_cols[0:WIDTH, at] = keep_ref[:, at]
        rows = lax.broadcasted_iota(jnp.int32, (DEPTH - WIDTH, TILE), 0)
        keep_cols[WIDTH:DEPTH, at] = jnp.where(rows < 3, 1.0, 0.0).astype(jnp.bfloat16)
        top[:, at] = jnp.full((8, TILE), LOWEST, jnp.float32)
        total[:, at] = jnp.zeros((8, TILE), jnp.float32)
        return 0

    lax.fori_loop(0, red_tiles, prepare_reduced, 0)
    lax.fori_loop(0, keep_tiles, prepare_kept, 0)

    lanes_of, rows_of = 256, 128

    def step(entry, _):
        red_at = pl.multiple_of(list_ref[red_row, entry] * TILE, TILE)
        keep_at = pl.multiple_of(list_ref[keep_row, entry] * TILE, TILE)
        for lane in range(0, TILE, lanes_of):
            lanes = pl.ds(pl.multiple_of(keep_at + lane, lanes_of), lanes_of)
            highest, summed = top[:, lanes], total[:, lanes]
            columns = keep_cols[:, lanes]
            for row in range(0, TILE, rows_of):
                block = red_rows[pl.ds(pl.multiple_of(red_at + row, rows_of), rows_of), :DEPTH]
                z = jnp.dot(block, columns, preferred_element_type=jnp.float32)
                z = z.reshape(rows_of // 8, 8, lanes_of)
                higher = jnp.maximum(highest, jnp.max(z, axis=0))
                summed = summed * scaled_exp(highest - higher) + jnp.sum(scaled_exp(z - higher[None]), axis=0)
                highest = higher
            top[:, lanes] = highest
            total[:, lanes] = summed
        return 0

    lax.fori_loop(0, count_ref[0, 0], step, 0)

    def finish(tile, _):
        at = at_tile(tile)
        highest = jnp.max(top[:, at], axis=0, keepdims=True)
        summed = jnp.sum(total[:, at] * scaled_exp(top[:, at] - highest), axis=0, keepdims=True)
        cells = keep_ref[:, at].astype(jnp.float32)
        half_square = 0.5 * jnp.sum(cells * cells, axis=0, keepdims=True)
        out_ref[:, at] = highest + jnp.log(jnp.maximum(summed, 1.0)) * (1.0 / UNIT) - half_square
        return 0

    lax.fori_loop(0, keep_tiles, finish, 0)


def block_lse(name, red_row, reduced, kept, bias, own_list, own_count):
    red_cells, keep_cells = reduced.shape[1], kept.shape[1]
    vmem = pl.BlockSpec(memory_space=pltpu.VMEM)
    smem = pl.BlockSpec(memory_space=pltpu.SMEM)
    return pl.pallas_call(
        functools.partial(lse_kernel, red_row, 1 - red_row),
        name=name,
        out_shape=jax.ShapeDtypeStruct((1, keep_cells), jnp.float32),
        in_specs=[smem, smem, vmem, vmem, vmem],
        out_specs=vmem,
        scratch_shapes=[
            pltpu.VMEM((red_cells, 128), jnp.bfloat16),
            pltpu.VMEM((DEPTH, keep_cells), jnp.bfloat16),
            pltpu.VMEM((8, keep_cells), jnp.float32),
            pltpu.VMEM((8, keep_cells), jnp.float32),
        ],
        compiler_params=pltpu.CompilerParams(vmem_limit_bytes=32 << 20),
    )(own_list, own_count, reduced, kept, bias)


def merged(parts):
    highest = functools.reduce(jnp.maximum, parts)
    summed = sum(jnp.exp(UNIT * (part - highest)) for part in parts)
    return highest + jnp.log(summed) * (1.0 / UNIT)


def along(axis, size, group, stride, shift):
    pairs = []
    for index in range(size):
        digit = index // stride % group
        pairs.append((index, index + ((digit + shift) % group - digit) * stride))
    return lambda value: lax.ppermute(value, axis, pairs)


def local(source_embed, target_embed, target_potential, log_source_mass, log_target_mass, tile_list, counts):
    sources = lax.axis_size("src")
    copies = jnp.broadcast_to(target_embed[None], (sources,) + target_embed.shape)
    target_full = lax.all_to_all(copies, "src", 0, 0).reshape(WIDTH, -1)
    source_full = lax.all_gather(source_embed, "tgt", axis=0, tiled=True)
    own_list = tile_list[0, 0]

    row = block_lse("row_lse", 1, target_full, source_full, target_potential[None], own_list, counts)
    row = merged([row, along("tgt", 8, 2, 1, 1)(row)])
    row = merged([row] + [along("tgt", 8, 4, 2, shift)(row) for shift in (1, 2, 3)])
    row_potential = EPSILON * log_source_mass[None] - row * (1.0 / HALF)

    column = block_lse("column_lse", 0, source_full, target_full, row_potential, own_list, counts)
    column = merged([column] + [along("src", 16, 4, 4, shift)(column) for shift in (1, 2, 3)])
    column = merged([column] + [along("src", 16, 4, 1, shift)(column) for shift in (1, 2, 3)])
    column_potential = EPSILON * log_target_mass[None] - column * (1.0 / HALF)
    return row_potential[0], column_potential[0]


def solution(mesh):
    return jax.shard_map(
        local,
        mesh=mesh,
        in_specs=(
            P("tgt", "src"),
            P("src", "tgt"),
            P("tgt"),
            P("src"),
            P("tgt"),
            P("src", "tgt", None, None),
            P("src", "tgt"),
        ),
        out_specs=(P("src"), P("tgt")),
        check_vma=False,
    )
```

```python
import functools

import jax
import jax.numpy as jnp
from jax import lax
from jax.experimental import pallas as pl
from jax.experimental.pallas import tpu as pltpu
from jax.sharding import PartitionSpec as P

TILE = 512
WIDTH = 32
DEPTH = 48
EPSILON = 0.1
HALF = float(WIDTH)
UNIT = 1.0 / (EPSILON * HALF)
ALPHA = UNIT * 1.4426950408889634
LOWEST = -1e30


def scaled_exp(value):
    return jnp.exp2(value * ALPHA)


def lse_kernel(red_row, keep_row, list_ref, count_ref, red_ref, keep_ref, bias_ref, out_ref, red_rows, keep_cols, top, total):
    red_tiles = red_ref.shape[1] // TILE
    keep_tiles = keep_ref.shape[1] // TILE

    def at_tile(tile):
        return pl.ds(pl.multiple_of(tile * TILE, TILE), TILE)

    def prepare_reduced(tile, _):
        at = at_tile(tile)
        cells = red_ref[:, at].astype(jnp.float32)
        bias = HALF * bias_ref[:, at] - 0.5 * jnp.sum(cells * cells, axis=0, keepdims=True)
        first = bias.astype(jnp.bfloat16).astype(jnp.float32)
        rest = bias - first
        second = rest.astype(jnp.bfloat16).astype(jnp.float32)
        filler = jnp.zeros((128 - WIDTH - 3, TILE), jnp.float32)
        rows = jnp.concatenate([cells, first, second, rest - second, filler], axis=0)
        red_rows[at, :] = jnp.transpose(rows).astype(jnp.bfloat16)
        return 0

    def prepare_kept(tile, _):
        at = at_tile(tile)
        keep_cols[0:WIDTH, at] = keep_ref[:, at]
        rows = lax.broadcasted_iota(jnp.int32, (DEPTH - WIDTH, TILE), 0)
        keep_cols[WIDTH:DEPTH, at] = jnp.where(rows < 3, 1.0, 0.0).astype(jnp.bfloat16)
        top[:, at] = jnp.full((8, TILE), LOWEST, jnp.float32)
        total[:, at] = jnp.zeros((8, TILE), jnp.float32)
        return 0

    lax.fori_loop(0, red_tiles, prepare_reduced, 0)
    lax.fori_loop(0, keep_tiles, prepare_kept, 0)

    lanes_of, rows_of, together = 512, 64, 4

    def step(entry, _):
        red_at = pl.multiple_of(list_ref[red_row, entry] * TILE, TILE)
        keep_at = pl.multiple_of(list_ref[keep_row, entry] * TILE, TILE)
        for lane in range(0, TILE, lanes_of):
            lanes = pl.ds(pl.multiple_of(keep_at + lane, lanes_of), lanes_of)
            highest, summed = top[:, lanes], total[:, lanes]
            columns = keep_cols[:, lanes]
            for row in range(0, TILE, rows_of):
                block = red_rows[pl.ds(pl.multiple_of(red_at + row, rows_of), rows_of), :DEPTH]
                z = jnp.dot(block, columns, preferred_element_type=jnp.float32)
                z = z.reshape(rows_of // 8, 8, lanes_of)
                higher = jnp.maximum(highest, jnp.max(z, axis=0))
                summed = summed * scaled_exp(highest - higher) + jnp.sum(scaled_exp(z - higher[None]), axis=0)
                highest = higher
            top[:, lanes] = highest
            total[:, lanes] = summed
        return 0

    def steps(group, _):
        for member in range(together):
            step(group * together + member, 0)
        return 0

    live = count_ref[0, 0]
    whole = live // together
    lax.fori_loop(0, whole, steps, 0)
    lax.fori_loop(whole * together, live, step, 0)

    def finish(tile, _):
        at = at_tile(tile)
        highest = jnp.max(top[:, at], axis=0, keepdims=True)
        summed = jnp.sum(total[:, at] * scaled_exp(top[:, at] - highest), axis=0, keepdims=True)
        cells = keep_ref[:, at].astype(jnp.float32)
        half_square = 0.5 * jnp.sum(cells * cells, axis=0, keepdims=True)
        out_ref[:, at] = highest + jnp.log(jnp.maximum(summed, 1.0)) * (1.0 / UNIT) - half_square
        return 0

    lax.fori_loop(0, keep_tiles, finish, 0)


def block_lse(name, red_row, reduced, kept, bias, own_list, own_count):
    red_cells, keep_cells = reduced.shape[1], kept.shape[1]
    vmem = pl.BlockSpec(memory_space=pltpu.VMEM)
    smem = pl.BlockSpec(memory_space=pltpu.SMEM)
    return pl.pallas_call(
        functools.partial(lse_kernel, red_row, 1 - red_row),
        name=name,
        out_shape=jax.ShapeDtypeStruct((1, keep_cells), jnp.float32),
        in_specs=[smem, smem, vmem, vmem, vmem],
        out_specs=vmem,
        scratch_shapes=[
            pltpu.VMEM((red_cells, 128), jnp.bfloat16),
            pltpu.VMEM((DEPTH, keep_cells), jnp.bfloat16),
            pltpu.VMEM((8, keep_cells), jnp.float32),
            pltpu.VMEM((8, keep_cells), jnp.float32),
        ],
        compiler_params=pltpu.CompilerParams(vmem_limit_bytes=32 << 20),
    )(own_list, own_count, reduced, kept, bias)


def merged(parts):
    highest = functools.reduce(jnp.maximum, parts)
    summed = sum(jnp.exp(UNIT * (part - highest)) for part in parts)
    return highest + jnp.log(summed) * (1.0 / UNIT)


def along(axis, size, group, stride, shift):
    pairs = []
    for index in range(size):
        digit = index // stride % group
        pairs.append((index, index + ((digit + shift) % group - digit) * stride))
    return lambda value: lax.ppermute(value, axis, pairs)


def local(source_embed, target_embed, target_potential, log_source_mass, log_target_mass, tile_list, counts):
    sources = lax.axis_size("src")
    copies = jnp.broadcast_to(target_embed[None], (sources,) + target_embed.shape)
    target_full = lax.all_to_all(copies, "src", 0, 0).reshape(WIDTH, -1)
    source_full = lax.all_gather(source_embed, "tgt", axis=0, tiled=True)
    own_list = tile_list[0, 0]

    row = block_lse("row_lse", 1, target_full, source_full, target_potential[None], own_list, counts)
    row = merged([row, along("tgt", 8, 2, 1, 1)(row)])
    row = merged([row] + [along("tgt", 8, 4, 2, shift)(row) for shift in (1, 2, 3)])
    row_potential = EPSILON * log_source_mass[None] - row * (1.0 / HALF)

    column = block_lse("column_lse", 0, source_full, target_full, row_potential, own_list, counts)
    column = merged([column] + [along("src", 16, 4, 4, shift)(column) for shift in (1, 2, 3)])
    column = merged([column] + [along("src", 16, 4, 1, shift)(column) for shift in (1, 2, 3)])
    column_potential = EPSILON * log_target_mass[None] - column * (1.0 / HALF)
    return row_potential[0], column_potential[0]


def solution(mesh):
    return jax.shard_map(
        local,
        mesh=mesh,
        in_specs=(
            P("tgt", "src"),
            P("src", "tgt"),
            P("tgt"),
            P("src"),
            P("tgt"),
            P("src", "tgt", None, None),
            P("src", "tgt"),
        ),
        out_specs=(P("src"), P("tgt")),
        check_vma=False,
    )
```

```python
import functools

import jax
import jax.numpy as jnp
from jax import lax
from jax.experimental import pallas as pl
from jax.experimental.pallas import tpu as pltpu
from jax.sharding import PartitionSpec as P

TILE = 512
WIDTH = 32
PIECES = 3
LEFT = 128
RIGHT = 112
DEPTH = 48
TOGETHER = 8
STORES = 4
EPSILON = 0.1
KAPPA = 1.4426950408889634 / EPSILON
ALPHA = KAPPA / WIDTH
GAMMA = KAPPA / (2 * WIDTH)
LOWEST = -1e30
TRUSTED = 2.0**-90

BF16, F32 = jnp.bfloat16, jnp.float32
VMEM = pl.BlockSpec(memory_space=pltpu.VMEM)
SMEM = pl.BlockSpec(memory_space=pltpu.SMEM)
ANY = pl.BlockSpec(memory_space=pl.ANY)


def at_tile(tile):
    return pl.ds(pl.multiple_of(tile * TILE, TILE), TILE)


def pieces(value, number=PIECES):
    terms = []
    for _ in range(number):
        terms.append(value.astype(BF16).astype(F32))
        value = value - terms[-1]
    return terms


def squares(cells):
    return jnp.sum(cells * cells, axis=0, keepdims=True)


def general_lse(red_row, keep_row, list_ref, live, red_ref, keep_ref, bias_ref, out_ref, top, total):
    keep_tiles = keep_ref.shape[1] // TILE
    half, scale = float(WIDTH), ALPHA
    rows_of = 64

    def clear(tile, _):
        at = at_tile(tile)
        top[:, at] = jnp.full((8, TILE), LOWEST, F32)
        total[:, at] = jnp.zeros((8, TILE), F32)
        return 0

    def step(entry, _):
        red_at = at_tile(list_ref[red_row, entry])
        keep_at = at_tile(list_ref[keep_row, entry])
        cells = red_ref[:, red_at].astype(F32)
        terms = pieces(half * bias_ref[:, red_at] - 0.5 * squares(cells))
        filler = jnp.zeros((DEPTH - WIDTH - PIECES, TILE), F32)
        left = jnp.transpose(jnp.concatenate([cells] + terms + [filler, jnp.zeros((LEFT - DEPTH, TILE), F32)], axis=0))
        left = left.astype(BF16)[:, :DEPTH]
        right = jnp.concatenate([keep_ref[:, keep_at].astype(F32), jnp.ones((PIECES, TILE), F32), filler], axis=0).astype(BF16)
        highest, summed = top[:, keep_at], total[:, keep_at]
        for row in range(0, TILE, rows_of):
            z = jnp.dot(left[row : row + rows_of], right, preferred_element_type=F32)
            z = z.reshape(rows_of // 8, 8, TILE) * scale
            higher = jnp.maximum(highest, jnp.max(z, axis=0))
            summed = summed * jnp.exp2(highest - higher) + jnp.sum(jnp.exp2(z - higher[None]), axis=0)
            highest = higher
        top[:, keep_at] = highest
        total[:, keep_at] = summed
        return 0

    def finish(tile, _):
        at = at_tile(tile)
        highest = jnp.max(top[:, at], axis=0, keepdims=True)
        summed = jnp.sum(total[:, at] * jnp.exp2(top[:, at] - highest), axis=0, keepdims=True)
        value = highest * (1.0 / KAPPA) + EPSILON * jnp.log(jnp.maximum(summed, 1.0))
        out_ref[:, at] = value - squares(keep_ref[:, at].astype(F32)) * (0.5 / WIDTH)
        return 0

    lax.fori_loop(0, keep_tiles, clear, 0)
    lax.fori_loop(0, live, step, 0)
    lax.fori_loop(0, keep_tiles, finish, 0)


def source_kernel(source_ref, left_ref):
    def prepare(tile, _):
        at = at_tile(tile)
        cells = source_ref[:, at].astype(F32)
        rows = pieces(cells * ALPHA) + [jnp.ones((PIECES, TILE), F32)] + pieces(squares(cells) * -GAMMA)
        rows.append(jnp.zeros((LEFT - PIECES * WIDTH - 2 * PIECES, TILE), F32))
        left_ref[at, :] = jnp.transpose(jnp.concatenate(rows, axis=0)).astype(BF16)
        return 0

    lax.fori_loop(0, source_ref.shape[1] // TILE, prepare, 0)


def groups(live, body):
    def one(group, _):
        for member in range(TOGETHER):
            entry = group * TOGETHER + member
            body(entry, member % STORES, entry // STORES)
        return 0

    lax.fori_loop(0, (live + TOGETHER - 1) // TOGETHER, one, 0)


def clear_marks(marks):
    for tile in range(marks.shape[0]):
        marks[tile] = 0


def row_kernel(
    list_ref, count_ref, left_ref, target_ref, potential_ref, source_hbm,
    out_ref, store_0, store_1, store_2, store_3,
    right, weight, sums, covered, smallest, top, total, source_ref, semaphore,
):
    stores = (store_0, store_1, store_2, store_3)
    source_tiles = left_ref.shape[0] // TILE
    target_tiles = target_ref.shape[1] // TILE
    live = count_ref[0, 0]
    highest = jnp.max(potential_ref[...], axis=1, keepdims=True)
    rows_of = 64

    def clear(tile, _):
        sums[at_tile(tile), :] = jnp.zeros((TILE, 128), F32)
        return 0

    def prepare(tile, _):
        at = at_tile(tile)
        cells = target_ref[:, at]
        for piece in range(PIECES):
            right[piece * WIDTH : (piece + 1) * WIDTH, at] = cells
        tail = pieces(squares(cells.astype(F32)) * -GAMMA) + [jnp.ones((PIECES, TILE), F32)]
        tail.append(jnp.zeros((RIGHT - PIECES * WIDTH - 2 * PIECES, TILE), F32))
        right[PIECES * WIDTH : RIGHT, at] = jnp.concatenate(tail, axis=0).astype(BF16)
        weight[:, at] = jnp.exp2((potential_ref[:, at] - highest) * KAPPA)
        return 0

    clear_marks(covered)
    lax.fori_loop(0, source_tiles, clear, 0)
    lax.fori_loop(0, target_tiles, prepare, 0)

    def step(entry, store, slot):
        alive = (entry < live).astype(jnp.int32)
        source_tile = list_ref[0, entry]
        target_at = at_tile(list_ref[1, entry])
        covered[source_tile] = jnp.maximum(covered[source_tile], alive)
        factor = weight[:, target_at] * alive.astype(F32)
        columns = right[:, target_at]
        for row in range(0, TILE, rows_of):
            at = pl.ds(pl.multiple_of(source_tile * TILE + row, rows_of), rows_of)
            value = jnp.exp2(jnp.dot(left_ref[at, :RIGHT], columns, preferred_element_type=F32))
            stores[store][slot, row : row + rows_of, :] = value.astype(BF16)
            value = value * factor
            sums[at, :] += (value[:, 0:128] + value[:, 128:256]) + (value[:, 256:384] + value[:, 384:512])

    groups(live, step)
    smallest[...] = jnp.ones((1, TILE), F32)

    def finish(tile, _):
        at = at_tile(tile)
        lines = sum(
            lax.dot_general(jnp.ones((16, 128), BF16), piece.astype(BF16), (((1,), (1,)), ((), ())), preferred_element_type=F32)
            for piece in pieces(sums[at, :], 2)
        )
        summed = lines[0:1]
        present = covered[tile] > 0
        value = highest + EPSILON * jnp.log(jnp.maximum(summed, TRUSTED))
        out_ref[:, at] = jnp.where(present, value, LOWEST)
        smallest[...] = jnp.minimum(smallest[...], jnp.where(present, summed, 1.0))
        return 0

    lax.fori_loop(0, source_tiles, finish, 0)

    @pl.when(jnp.min(smallest[...]) < TRUSTED)
    def _():
        copy = pltpu.make_async_copy(source_hbm, source_ref, semaphore)
        copy.start()
        copy.wait()
        general_lse(1, 0, list_ref, live, target_ref, source_ref, potential_ref, out_ref, top, total)


def column_kernel(
    list_ref, count_ref, potential_ref, store_0, store_1, store_2, store_3, source_hbm, target_hbm,
    out_ref,
    weight, sums, covered, smallest, top, total, source_ref, target_ref, semaphore,
):
    stores = (store_0, store_1, store_2, store_3)
    source_tiles = source_ref.shape[1] // TILE
    target_tiles = target_ref.shape[1] // TILE
    live = count_ref[0, 0]
    highest = jnp.max(potential_ref[...], axis=1, keepdims=True)

    def prepare(tile, _):
        at = at_tile(tile)
        terms = pieces(jnp.exp2((potential_ref[:, at] - highest) * KAPPA))
        weight[:, at] = jnp.concatenate(terms + [jnp.zeros((16 - PIECES, TILE), F32)], axis=0).astype(BF16)
        return 0

    def clear(tile, _):
        sums[:, at_tile(tile)] = jnp.zeros((16, TILE), F32)
        return 0

    clear_marks(covered)
    lax.fori_loop(0, source_tiles, prepare, 0)
    lax.fori_loop(0, target_tiles, clear, 0)

    def step(entry, store, slot):
        alive = (entry < live).astype(jnp.int32)
        target_tile = list_ref[1, entry]
        covered[target_tile] = jnp.maximum(covered[target_tile], alive)
        lines = jnp.dot(weight[:, at_tile(list_ref[0, entry])], stores[store][slot], preferred_element_type=F32)
        sums[:, at_tile(target_tile)] += lines * alive.astype(F32)

    groups(live, step)
    smallest[...] = jnp.ones((1, TILE), F32)

    def finish(tile, _):
        at = at_tile(tile)
        summed = jnp.sum(sums[:, at], axis=0, keepdims=True)
        present = covered[tile] > 0
        value = highest + EPSILON * jnp.log(jnp.maximum(summed, TRUSTED))
        out_ref[:, at] = jnp.where(present, value, LOWEST)
        smallest[...] = jnp.minimum(smallest[...], jnp.where(present, summed, 1.0))
        return 0

    lax.fori_loop(0, target_tiles, finish, 0)

    @pl.when(jnp.min(smallest[...]) < TRUSTED)
    def _():
        for hbm, ref in ((source_hbm, source_ref), (target_hbm, target_ref)):
            copy = pltpu.make_async_copy(hbm, ref, semaphore)
            copy.start()
            copy.wait()
        general_lse(0, 1, list_ref, live, source_ref, target_ref, potential_ref, out_ref, top, total)


def merged(parts):
    highest = functools.reduce(jnp.maximum, parts)
    summed = sum(jnp.exp((part - highest) * (1.0 / EPSILON)) for part in parts)
    return highest + EPSILON * jnp.log(summed)


def along(axis, size, group, stride, shift):
    pairs = []
    for index in range(size):
        digit = index // stride % group
        pairs.append((index, index + ((digit + shift) % group - digit) * stride))
    return lambda value: lax.ppermute(value, axis, pairs)


def local(source_embed, target_embed, target_potential, log_source_mass, log_target_mass, tile_list, counts):
    sources = lax.axis_size("src")
    copies = jnp.broadcast_to(target_embed[None], (sources,) + target_embed.shape)
    target_full = lax.all_to_all(copies, "src", 0, 0).reshape(WIDTH, -1)
    source_full = lax.all_gather(source_embed, "tgt", axis=0, tiled=True)
    own_list = tile_list[0, 0]
    source_cells, target_cells = source_full.shape[1], target_full.shape[1]
    slots = own_list.shape[1] // STORES

    left = pl.pallas_call(
        source_kernel,
        name="source_side",
        out_shape=pltpu.VMEM((source_cells, LEFT), BF16),
        in_specs=[VMEM],
        out_specs=VMEM,
        compiler_params=pltpu.CompilerParams(vmem_limit_bytes=10 << 20),
    )(source_full)

    row, *stores = pl.pallas_call(
        row_kernel,
        name="row_sums",
        out_shape=(jax.ShapeDtypeStruct((1, source_cells), F32),) + (pltpu.VMEM((slots, TILE, TILE), BF16),) * STORES,
        in_specs=[SMEM, SMEM, VMEM, VMEM, VMEM, ANY],
        out_specs=(VMEM,) * (1 + STORES),
        scratch_shapes=[
            pltpu.VMEM((RIGHT, target_cells), BF16),
            pltpu.VMEM((1, target_cells), F32),
            pltpu.VMEM((source_cells, 128), F32),
            pltpu.SMEM((source_cells // TILE,), jnp.int32),
            pltpu.VMEM((1, TILE), F32),
            pltpu.VMEM((8, source_cells), F32),
            pltpu.VMEM((8, source_cells), F32),
            pltpu.VMEM((WIDTH, source_cells), BF16),
            pltpu.SemaphoreType.DMA,
        ],
        compiler_params=pltpu.CompilerParams(vmem_limit_bytes=12 << 20),
    )(own_list, counts, left, target_full, target_potential[None], source_full)

    row = merged([row, along("tgt", 8, 2, 1, 1)(row)])
    row = merged([row] + [along("tgt", 8, 4, 2, shift)(row) for shift in (1, 2, 3)])
    row_potential = EPSILON * log_source_mass[None] - row

    column = pl.pallas_call(
        column_kernel,
        name="column_sums",
        out_shape=jax.ShapeDtypeStruct((1, target_cells), F32),
        in_specs=[SMEM, SMEM, VMEM] + [VMEM] * STORES + [ANY, ANY],
        out_specs=VMEM,
        scratch_shapes=[
            pltpu.VMEM((16, source_cells), BF16),
            pltpu.VMEM((16, target_cells), F32),
            pltpu.SMEM((target_cells // TILE,), jnp.int32),
            pltpu.VMEM((1, TILE), F32),
            pltpu.VMEM((8, target_cells), F32),
            pltpu.VMEM((8, target_cells), F32),
            pltpu.VMEM((WIDTH, source_cells), BF16),
            pltpu.VMEM((WIDTH, target_cells), BF16),
            pltpu.SemaphoreType.DMA,
        ],
        compiler_params=pltpu.CompilerParams(vmem_limit_bytes=10 << 20),
    )(own_list, counts, row_potential, *stores, source_full, target_full)

    column = merged([column] + [along("src", 16, 4, 4, shift)(column) for shift in (1, 2, 3)])
    column = merged([column] + [along("src", 16, 4, 1, shift)(column) for shift in (1, 2, 3)])
    column_potential = EPSILON * log_target_mass[None] - column
    return row_potential[0], column_potential[0]


def solution(mesh):
    return jax.shard_map(
        local,
        mesh=mesh,
        in_specs=(
            P("tgt", "src"),
            P("src", "tgt"),
            P("tgt"),
            P("src"),
            P("tgt"),
            P("src", "tgt", None, None),
            P("src", "tgt"),
        ),
        out_specs=(P("src"), P("tgt")),
        check_vma=False,
    )
```

```python
import functools

import jax
import jax.numpy as jnp
from jax import lax
from jax.experimental import pallas as pl
from jax.experimental.pallas import tpu as pltpu
from jax.sharding import PartitionSpec as P

TILE = 512
LINES = TILE // 128
WIDTH = 32
PIECES = 3
LEFT = 128
RIGHT = 112
DEPTH = 48
TOGETHER = 16
UNROLL = 4
STORES = 4
EPSILON = 0.1
KAPPA = 1.4426950408889634 / EPSILON
ALPHA = KAPPA / WIDTH
GAMMA = KAPPA / (2 * WIDTH)
LOWEST = -1e30
TRUSTED = 2.0**-90

BF16, F32 = jnp.bfloat16, jnp.float32
VMEM = pl.BlockSpec(memory_space=pltpu.VMEM)
SMEM = pl.BlockSpec(memory_space=pltpu.SMEM)
ANY = pl.BlockSpec(memory_space=pl.ANY)
HBM = pl.BlockSpec(memory_space=pltpu.HBM)


def at_tile(tile):
    return pl.ds(pl.multiple_of(tile * TILE, TILE), TILE)


def write_line(ref, tile, line):
    for part in range(LINES):
        ref[pl.ds(tile * LINES + part, 1), :] = line[:, part * 128 : (part + 1) * 128]


def read_line(ref, tile):
    return jnp.concatenate([ref[pl.ds(tile * LINES + part, 1), :] for part in range(LINES)], axis=1)


def highest_of(ref):
    return jnp.max(jnp.max(ref[...], axis=0, keepdims=True), axis=1, keepdims=True)


def pieces(value, number=PIECES):
    terms = []
    for _ in range(number):
        terms.append(value.astype(BF16).astype(F32))
        value = value - terms[-1]
    return terms


def squares(cells):
    return jnp.sum(cells * cells, axis=0, keepdims=True)


def general_lse(red_row, keep_row, list_ref, live, read_red, read_keep, read_bias, out_ref, top, total):
    keep_tiles = top.shape[1] // TILE
    half, scale = float(WIDTH), ALPHA
    rows_of = 64

    def clear(tile, _):
        at = at_tile(tile)
        top[:, at] = jnp.full((8, TILE), LOWEST, F32)
        total[:, at] = jnp.zeros((8, TILE), F32)
        return 0

    def step(entry, _):
        red_tile, keep_tile = list_ref[red_row, entry], list_ref[keep_row, entry]
        keep_at = at_tile(keep_tile)
        cells = read_red(red_tile)
        terms = pieces(half * read_bias(red_tile) - 0.5 * squares(cells))
        filler = jnp.zeros((DEPTH - WIDTH - PIECES, TILE), F32)
        left = jnp.transpose(jnp.concatenate([cells] + terms + [filler, jnp.zeros((LEFT - DEPTH, TILE), F32)], axis=0))
        left = left.astype(BF16)[:, :DEPTH]
        right = jnp.concatenate([read_keep(keep_tile), jnp.ones((PIECES, TILE), F32), filler], axis=0).astype(BF16)
        highest, summed = top[:, keep_at], total[:, keep_at]
        for row in range(0, TILE, rows_of):
            z = jnp.dot(left[row : row + rows_of], right, preferred_element_type=F32)
            z = z.reshape(rows_of // 8, 8, TILE) * scale
            higher = jnp.maximum(highest, jnp.max(z, axis=0))
            summed = summed * jnp.exp2(highest - higher) + jnp.sum(jnp.exp2(z - higher[None]), axis=0)
            highest = higher
        top[:, keep_at] = highest
        total[:, keep_at] = summed
        return 0

    def finish(tile, _):
        at = at_tile(tile)
        highest = jnp.max(top[:, at], axis=0, keepdims=True)
        summed = jnp.sum(total[:, at] * jnp.exp2(top[:, at] - highest), axis=0, keepdims=True)
        value = highest * (1.0 / KAPPA) + EPSILON * jnp.log(jnp.maximum(summed, 1.0))
        write_line(out_ref, tile, value - squares(read_keep(tile)) * (0.5 / WIDTH))
        return 0

    lax.fori_loop(0, keep_tiles, clear, 0)
    lax.fori_loop(0, live, step, 0)
    lax.fori_loop(0, keep_tiles, finish, 0)


def copies_kernel(part_ref, copies_ref):
    for copy in range(copies_ref.shape[0]):
        copies_ref[copy] = part_ref[...]


def source_kernel(source_ref, left_ref):
    def prepare(tile, _):
        at = at_tile(tile)
        cells = source_ref[:, at].astype(F32)
        rows = pieces(cells * ALPHA) + [jnp.ones((PIECES, TILE), F32)] + pieces(squares(cells) * -GAMMA)
        rows.append(jnp.zeros((LEFT - PIECES * WIDTH - 2 * PIECES, TILE), F32))
        left_ref[at, :] = jnp.transpose(jnp.concatenate(rows, axis=0)).astype(BF16)
        return 0

    lax.fori_loop(0, source_ref.shape[1] // TILE, prepare, 0, unroll=UNROLL)


def groups(live, body):
    def one(group, _):
        for member in range(TOGETHER):
            entry = group * TOGETHER + member
            body(entry, member % STORES, entry // STORES)
        return 0

    lax.fori_loop(0, (live + TOGETHER - 1) // TOGETHER, one, 0)


def clear_marks(marks):
    for tile in range(marks.shape[0]):
        marks[tile] = 0


def row_kernel(
    list_ref, count_ref, left_hbm, target_ref, potential_ref, source_hbm,
    out_ref, store_0, store_1, store_2, store_3,
    left_ref, right, weight, sums, covered, smallest, top, total, source_ref, semaphores,
):
    stores = (store_0, store_1, store_2, store_3)
    source_tiles = left_ref.shape[0] // TILE
    target_tiles = right.shape[1] // TILE
    live = count_ref[0, 0]
    fetch = pltpu.make_async_copy(left_hbm, left_ref, semaphores.at[0])
    fetch.start()
    highest = highest_of(potential_ref)
    rows_of = 64

    def prepare(tile, _):
        at = at_tile(tile)
        cells = target_ref[:, at]
        for piece in range(PIECES):
            right[piece * WIDTH : (piece + 1) * WIDTH, at] = cells
        tail = pieces(squares(cells.astype(F32)) * -GAMMA) + [jnp.ones((PIECES, TILE), F32)]
        tail.append(jnp.zeros((RIGHT - PIECES * WIDTH - 2 * PIECES, TILE), F32))
        right[PIECES * WIDTH : RIGHT, at] = jnp.concatenate(tail, axis=0).astype(BF16)
        weight[:, at] = jnp.exp2((read_line(potential_ref, tile) - highest) * KAPPA)
        share = sums.shape[0] // target_tiles
        sums[pl.ds(pl.multiple_of(tile * share, share), share), :] = jnp.zeros((share, 128), F32)
        return 0

    clear_marks(covered)
    lax.fori_loop(0, target_tiles, prepare, 0, unroll=UNROLL)
    fetch.wait()

    def step(entry, store, slot):
        alive = (entry < live).astype(jnp.int32)
        source_tile = list_ref[0, entry]
        target_at = at_tile(list_ref[1, entry])
        covered[source_tile] = jnp.maximum(covered[source_tile], alive)
        factor = weight[:, target_at] * alive.astype(F32)
        columns = right[:, target_at]
        for row in range(0, TILE, rows_of):
            at = pl.ds(pl.multiple_of(source_tile * TILE + row, rows_of), rows_of)
            value = jnp.exp2(jnp.dot(left_ref[at, :RIGHT], columns, preferred_element_type=F32))
            stores[store][slot, row : row + rows_of, :] = value.astype(BF16)
            value = value * factor
            sums[at, :] += (value[:, 0:128] + value[:, 128:256]) + (value[:, 256:384] + value[:, 384:512])

    groups(live, step)
    smallest[...] = jnp.ones((1, TILE), F32)

    def finish(tile, _):
        lines = sum(
            lax.dot_general(jnp.ones((16, 128), BF16), piece.astype(BF16), (((1,), (1,)), ((), ())), preferred_element_type=F32)
            for piece in pieces(sums[at_tile(tile), :], 2)
        )
        summed = lines[0:1]
        present = covered[tile] > 0
        value = highest + EPSILON * jnp.log(jnp.maximum(summed, TRUSTED))
        write_line(out_ref, tile, jnp.where(present, value, LOWEST))
        smallest[...] = jnp.minimum(smallest[...], jnp.where(present, summed, 1.0))
        return 0

    lax.fori_loop(0, source_tiles, finish, 0, unroll=UNROLL)

    @pl.when(jnp.min(smallest[...]) < TRUSTED)
    def _():
        copy = pltpu.make_async_copy(source_hbm, source_ref, semaphores.at[1])
        copy.start()
        copy.wait()
        general_lse(
            1, 0, list_ref, live,
            lambda tile: target_ref[:, at_tile(tile)].astype(F32),
            lambda tile: source_ref[:, at_tile(tile)].astype(F32),
            lambda tile: read_line(potential_ref, tile),
            out_ref, top, total,
        )


def column_kernel(
    list_ref, count_ref, potential_ref, store_0, store_1, store_2, store_3, source_hbm, target_hbm,
    out_ref,
    weight, sums, covered, smallest, top, total, source_ref, target_ref, semaphore,
):
    stores = (store_0, store_1, store_2, store_3)
    source_tiles = source_ref.shape[1] // TILE
    target_tiles = sums.shape[1] // TILE
    live = count_ref[0, 0]
    highest = highest_of(potential_ref)

    def prepare(tile, _):
        terms = pieces(jnp.exp2((read_line(potential_ref, tile) - highest) * KAPPA))
        weight[:, at_tile(tile)] = jnp.concatenate(terms + [jnp.zeros((16 - PIECES, TILE), F32)], axis=0).astype(BF16)
        return 0

    def clear(tile, _):
        sums[:, at_tile(tile)] = jnp.zeros((16, TILE), F32)
        return 0

    clear_marks(covered)
    lax.fori_loop(0, source_tiles, prepare, 0, unroll=UNROLL)
    lax.fori_loop(0, target_tiles, clear, 0, unroll=UNROLL)

    def step(entry, store, slot):
        alive = (entry < live).astype(jnp.int32)
        target_tile = list_ref[1, entry]
        covered[target_tile] = jnp.maximum(covered[target_tile], alive)
        lines = jnp.dot(weight[:, at_tile(list_ref[0, entry])], stores[store][slot], preferred_element_type=F32)
        sums[:, at_tile(target_tile)] += lines * alive.astype(F32)

    groups(live, step)
    smallest[...] = jnp.ones((1, TILE), F32)

    def finish(tile, _):
        summed = jnp.sum(sums[:, at_tile(tile)], axis=0, keepdims=True)
        present = covered[tile] > 0
        value = highest + EPSILON * jnp.log(jnp.maximum(summed, TRUSTED))
        write_line(out_ref, tile, jnp.where(present, value, LOWEST))
        smallest[...] = jnp.minimum(smallest[...], jnp.where(present, summed, 1.0))
        return 0

    lax.fori_loop(0, target_tiles, finish, 0, unroll=UNROLL)

    @pl.when(jnp.min(smallest[...]) < TRUSTED)
    def _():
        for hbm, ref in ((source_hbm, source_ref), (target_hbm, target_ref)):
            copy = pltpu.make_async_copy(hbm, ref, semaphore)
            copy.start()
            copy.wait()
        general_lse(
            0, 1, list_ref, live,
            lambda tile: source_ref[:, at_tile(tile)].astype(F32),
            lambda tile: target_ref[:, at_tile(tile)].astype(F32),
            lambda tile: read_line(potential_ref, tile),
            out_ref, top, total,
        )


def merged(parts):
    highest = functools.reduce(jnp.maximum, parts)
    summed = sum(jnp.exp((part - highest) * (1.0 / EPSILON)) for part in parts)
    return highest + EPSILON * jnp.log(summed)


def along(axis, size, group, stride, shift):
    pairs = []
    for index in range(size):
        digit = index // stride % group
        pairs.append((index, index + ((digit + shift) % group - digit) * stride))
    return lambda value: lax.ppermute(value, axis, pairs)


def local(source_embed, target_embed, target_potential, log_source_mass, log_target_mass, tile_list, counts):
    over_x = [along("src", 16, 4, 4, shift) for shift in (1, 2, 3)]
    over_z = [along("src", 16, 4, 1, shift) for shift in (1, 2, 3)]
    over_y = [along("tgt", 8, 4, 2, shift) for shift in (1, 2, 3)]
    over_core = along("tgt", 8, 2, 1, 1)

    sources = lax.axis_size("src")
    copies = pl.pallas_call(
        copies_kernel,
        name="target_copies",
        out_shape=pltpu.VMEM((sources,) + target_embed.shape, BF16),
        in_specs=[VMEM],
        out_specs=VMEM,
        compiler_params=pltpu.CompilerParams(vmem_limit_bytes=8 << 20),
    )(target_embed)
    target_full = lax.all_to_all(copies, "src", 0, 0).reshape(WIDTH, -1)
    source_full = lax.all_gather(source_embed, "tgt", axis=0, tiled=True)

    own_list = tile_list[0, 0]
    source_cells, target_cells = source_embed.shape[1], target_embed.shape[1]
    slots = own_list.shape[1] // STORES

    left = pl.pallas_call(
        source_kernel,
        name="source_side",
        out_shape=pltpu.HBM((source_cells, LEFT), BF16),
        in_specs=[VMEM],
        out_specs=VMEM,
        compiler_params=pltpu.CompilerParams(vmem_limit_bytes=10 << 20),
    )(source_full)

    row, *stores = pl.pallas_call(
        row_kernel,
        name="row_sums",
        out_shape=(jax.ShapeDtypeStruct((source_cells // 128, 128), F32),)
        + (pltpu.VMEM((slots, TILE, TILE), BF16),) * STORES,
        in_specs=[SMEM, SMEM, HBM, VMEM, VMEM, ANY],
        out_specs=(VMEM,) * (1 + STORES),
        scratch_shapes=[
            pltpu.VMEM((source_cells, LEFT), BF16),
            pltpu.VMEM((RIGHT, target_cells), BF16),
            pltpu.VMEM((1, target_cells), F32),
            pltpu.VMEM((source_cells, 128), F32),
            pltpu.SMEM((source_cells // TILE,), jnp.int32),
            pltpu.VMEM((1, TILE), F32),
            pltpu.VMEM((8, source_cells), F32),
            pltpu.VMEM((8, source_cells), F32),
            pltpu.VMEM((WIDTH, source_cells), BF16),
            pltpu.SemaphoreType.DMA((2,)),
        ],
        compiler_params=pltpu.CompilerParams(vmem_limit_bytes=14 << 20),
    )(own_list, counts, pltpu.with_memory_space_constraint(left, pltpu.HBM), target_full, target_potential.reshape(-1, 128), source_full)

    row = merged([row, over_core(row)])
    row = merged([row] + [send(row) for send in over_y])
    row_potential = EPSILON * log_source_mass.reshape(-1, 128) - row

    column = pl.pallas_call(
        column_kernel,
        name="column_sums",
        out_shape=jax.ShapeDtypeStruct((target_cells // 128, 128), F32),
        in_specs=[SMEM, SMEM, VMEM] + [VMEM] * STORES + [ANY, ANY],
        out_specs=VMEM,
        scratch_shapes=[
            pltpu.VMEM((16, source_cells), BF16),
            pltpu.VMEM((16, target_cells), F32),
            pltpu.SMEM((target_cells // TILE,), jnp.int32),
            pltpu.VMEM((1, TILE), F32),
            pltpu.VMEM((8, target_cells), F32),
            pltpu.VMEM((8, target_cells), F32),
            pltpu.VMEM((WIDTH, source_cells), BF16),
            pltpu.VMEM((WIDTH, target_cells), BF16),
            pltpu.SemaphoreType.DMA,
        ],
        compiler_params=pltpu.CompilerParams(vmem_limit_bytes=10 << 20),
    )(own_list, counts, row_potential, *stores, source_full, target_full)

    column = merged([column] + [send(column) for send in over_x])
    column = merged([column] + [send(column) for send in over_z])
    column_potential = EPSILON * log_target_mass.reshape(-1, 128) - column
    return row_potential.reshape(-1), column_potential.reshape(-1)


def solution(mesh):
    return jax.shard_map(
        local,
        mesh=mesh,
        in_specs=(
            P("tgt", "src"),
            P("src", "tgt"),
            P("tgt"),
            P("src"),
            P("tgt"),
            P("src", "tgt", None, None),
            P("src", "tgt"),
        ),
        out_specs=(P("src"), P("tgt")),
        check_vma=False,
    )
```

```python
import functools

import jax
import jax.numpy as jnp
from jax import lax
from jax.experimental import pallas as pl
from jax.experimental.pallas import tpu as pltpu
from jax.sharding import PartitionSpec as P

TILE = 512
LINES = TILE // 128
WIDTH = 32
PIECES = 3
LEFT = 128
RIGHT = 112
DEPTH = 48
TOGETHER = 16
UNROLL = 8
STORES = 4
EPSILON = 0.1
KAPPA = 1.4426950408889634 / EPSILON
ALPHA = KAPPA / WIDTH
GAMMA = KAPPA / (2 * WIDTH)
LOWEST = -1e30
TRUSTED = 2.0**-90

BF16, F32 = jnp.bfloat16, jnp.float32
VMEM = pl.BlockSpec(memory_space=pltpu.VMEM)
SMEM = pl.BlockSpec(memory_space=pltpu.SMEM)
HBM = pl.BlockSpec(memory_space=pltpu.HBM)


def in_hbm(value):
    return pltpu.with_memory_space_constraint(value, pltpu.HBM)


def at_tile(tile):
    return pl.ds(pl.multiple_of(tile * TILE, TILE), TILE)


def write_line(ref, tile, line):
    for part in range(LINES):
        ref[pl.ds(tile * LINES + part, 1), :] = line[:, part * 128 : (part + 1) * 128]


def read_line(ref, tile):
    return jnp.concatenate([ref[pl.ds(tile * LINES + part, 1), :] for part in range(LINES)], axis=1)


def highest_of(ref):
    return jnp.max(jnp.max(ref[...], axis=0, keepdims=True), axis=1, keepdims=True)


def pieces(value, number=PIECES):
    terms = []
    for _ in range(number):
        terms.append(value.astype(BF16).astype(F32))
        value = value - terms[-1]
    return terms


def squares(cells):
    return jnp.sum(cells * cells, axis=0, keepdims=True)


def general_lse(red_row, keep_row, list_ref, live, read_red, read_keep, read_bias, out_ref, top, total):
    keep_tiles = top.shape[1] // TILE
    half, scale = float(WIDTH), ALPHA
    rows_of = 64

    def clear(tile, _):
        at = at_tile(tile)
        top[:, at] = jnp.full((8, TILE), LOWEST, F32)
        total[:, at] = jnp.zeros((8, TILE), F32)
        return 0

    def step(entry, _):
        red_tile, keep_tile = list_ref[red_row, entry], list_ref[keep_row, entry]
        keep_at = at_tile(keep_tile)
        cells = read_red(red_tile)
        terms = pieces(half * read_bias(red_tile) - 0.5 * squares(cells))
        filler = jnp.zeros((DEPTH - WIDTH - PIECES, TILE), F32)
        left = jnp.transpose(jnp.concatenate([cells] + terms + [filler, jnp.zeros((LEFT - DEPTH, TILE), F32)], axis=0))
        left = left.astype(BF16)[:, :DEPTH]
        right = jnp.concatenate([read_keep(keep_tile), jnp.ones((PIECES, TILE), F32), filler], axis=0).astype(BF16)
        highest, summed = top[:, keep_at], total[:, keep_at]
        for row in range(0, TILE, rows_of):
            z = jnp.dot(left[row : row + rows_of], right, preferred_element_type=F32)
            z = z.reshape(rows_of // 8, 8, TILE) * scale
            higher = jnp.maximum(highest, jnp.max(z, axis=0))
            summed = summed * jnp.exp2(highest - higher) + jnp.sum(jnp.exp2(z - higher[None]), axis=0)
            highest = higher
        top[:, keep_at] = highest
        total[:, keep_at] = summed
        return 0

    def finish(tile, _):
        at = at_tile(tile)
        highest = jnp.max(top[:, at], axis=0, keepdims=True)
        summed = jnp.sum(total[:, at] * jnp.exp2(top[:, at] - highest), axis=0, keepdims=True)
        value = highest * (1.0 / KAPPA) + EPSILON * jnp.log(jnp.maximum(summed, 1.0))
        write_line(out_ref, tile, value - squares(read_keep(tile)) * (0.5 / WIDTH))
        return 0

    lax.fori_loop(0, keep_tiles, clear, 0)
    lax.fori_loop(0, live, step, 0)
    lax.fori_loop(0, keep_tiles, finish, 0)


def copies_kernel(part_ref, copies_ref):
    for copy in range(copies_ref.shape[0]):
        copies_ref[copy] = part_ref[...]


def source_rows(cells):
    rows = pieces(cells * ALPHA) + [jnp.ones((PIECES, TILE), F32)] + pieces(squares(cells) * -GAMMA)
    rows.append(jnp.zeros((LEFT - PIECES * WIDTH - 2 * PIECES, TILE), F32))
    return jnp.transpose(jnp.concatenate(rows, axis=0)).astype(BF16)


def groups(live, body):
    def one(group, _):
        for member in range(TOGETHER):
            entry = group * TOGETHER + member
            body(entry, member % STORES, entry // STORES)
        return 0

    lax.fori_loop(0, (live + TOGETHER - 1) // TOGETHER, one, 0)


def clear_marks(marks):
    for tile in range(marks.shape[0]):
        marks[tile] = 0


def row_kernel(
    list_hbm, count_ref, source_ref, target_ref, potential_hbm,
    out_ref, source_hbm, target_hbm, store_0, store_1, store_2, store_3,
    left_ref, right, weight, sums, covered, smallest, top, total, list_ref, potential_ref, semaphores,
):
    stores = (store_0, store_1, store_2, store_3)
    source_tiles = left_ref.shape[0] // TILE
    target_tiles = right.shape[1] // TILE
    live = count_ref[0, 0]
    rows_of = 64
    fetched = [
        pltpu.make_async_copy(potential_hbm, potential_ref, semaphores.at[2]),
        pltpu.make_async_copy(list_hbm, list_ref, semaphores.at[3]),
    ]
    for copy in fetched:
        copy.start()
    kept = [
        pltpu.make_async_copy(source_ref, source_hbm, semaphores.at[0]),
        pltpu.make_async_copy(target_ref, target_hbm, semaphores.at[1]),
    ]
    for copy in kept:
        copy.start()

    def prepare_source(tile, _):
        at = at_tile(tile)
        left_ref[at, :] = source_rows(source_ref[:, at].astype(F32))
        return 0

    clear_marks(covered)
    lax.fori_loop(0, source_tiles, prepare_source, 0, unroll=UNROLL)
    for copy in fetched:
        copy.wait()
    highest = highest_of(potential_ref)

    def prepare(tile, _):
        at = at_tile(tile)
        cells = target_ref[:, at]
        for piece in range(PIECES):
            right[piece * WIDTH : (piece + 1) * WIDTH, at] = cells
        tail = pieces(squares(cells.astype(F32)) * -GAMMA) + [jnp.ones((PIECES, TILE), F32)]
        tail.append(jnp.zeros((RIGHT - PIECES * WIDTH - 2 * PIECES, TILE), F32))
        right[PIECES * WIDTH : RIGHT, at] = jnp.concatenate(tail, axis=0).astype(BF16)
        weight[:, at] = jnp.exp2((read_line(potential_ref, tile) - highest) * KAPPA)
        share = sums.shape[0] // target_tiles
        sums[pl.ds(pl.multiple_of(tile * share, share), share), :] = jnp.zeros((share, 128), F32)
        return 0

    lax.fori_loop(0, target_tiles, prepare, 0, unroll=UNROLL)

    def step(entry, store, slot):
        alive = (entry < live).astype(jnp.int32)
        source_tile = list_ref[0, entry]
        target_at = at_tile(list_ref[1, entry])
        covered[source_tile] = jnp.maximum(covered[source_tile], alive)
        factor = weight[:, target_at] * alive.astype(F32)
        columns = right[:, target_at]
        for row in range(0, TILE, rows_of):
            at = pl.ds(pl.multiple_of(source_tile * TILE + row, rows_of), rows_of)
            value = jnp.exp2(jnp.dot(left_ref[at, :RIGHT], columns, preferred_element_type=F32))
            stores[store][slot, row : row + rows_of, :] = value.astype(BF16)
            value = value * factor
            sums[at, :] += (value[:, 0:128] + value[:, 128:256]) + (value[:, 256:384] + value[:, 384:512])

    groups(live, step)
    smallest[...] = jnp.ones((1, TILE), F32)

    def finish(tile, _):
        terms = jnp.concatenate(pieces(sums[at_tile(tile), :], 2), axis=1).astype(BF16)
        lines = lax.dot_general(jnp.ones((16, 256), BF16), terms, (((1,), (1,)), ((), ())), preferred_element_type=F32)
        summed = lines[0:1]
        present = covered[tile] > 0
        value = highest + EPSILON * jnp.log(jnp.maximum(summed, TRUSTED))
        write_line(out_ref, tile, jnp.where(present, value, LOWEST))
        smallest[...] = jnp.minimum(smallest[...], jnp.where(present, summed, 1.0))
        return 0

    lax.fori_loop(0, source_tiles, finish, 0, unroll=UNROLL)

    for copy in kept:
        copy.wait()

    @pl.when(jnp.min(smallest[...]) < TRUSTED)
    def _():
        general_lse(
            1, 0, list_ref, live,
            lambda tile: target_ref[:, at_tile(tile)].astype(F32),
            lambda tile: source_ref[:, at_tile(tile)].astype(F32),
            lambda tile: read_line(potential_ref, tile),
            out_ref, top, total,
        )


def column_kernel(
    list_hbm, count_ref, potential_ref, store_0, store_1, store_2, store_3, source_hbm, target_hbm,
    out_ref,
    weight, sums, covered, smallest, top, total, source_ref, target_ref, list_ref, semaphore,
):
    stores = (store_0, store_1, store_2, store_3)
    source_tiles = source_ref.shape[1] // TILE
    target_tiles = sums.shape[1] // TILE
    live = count_ref[0, 0]
    fetch = pltpu.make_async_copy(list_hbm, list_ref, semaphore)
    fetch.start()
    highest = highest_of(potential_ref)

    def prepare(tile, _):
        terms = pieces(jnp.exp2((read_line(potential_ref, tile) - highest) * KAPPA))
        weight[:, at_tile(tile)] = jnp.concatenate(terms + [jnp.zeros((16 - PIECES, TILE), F32)], axis=0).astype(BF16)
        return 0

    def clear(tile, _):
        sums[:, at_tile(tile)] = jnp.zeros((16, TILE), F32)
        return 0

    clear_marks(covered)
    lax.fori_loop(0, source_tiles, prepare, 0, unroll=UNROLL)
    lax.fori_loop(0, target_tiles, clear, 0, unroll=UNROLL)
    fetch.wait()

    def step(entry, store, slot):
        alive = (entry < live).astype(jnp.int32)
        target_tile = list_ref[1, entry]
        covered[target_tile] = jnp.maximum(covered[target_tile], alive)
        lines = jnp.dot(weight[:, at_tile(list_ref[0, entry])], stores[store][slot], preferred_element_type=F32)
        sums[:, at_tile(target_tile)] += lines * alive.astype(F32)

    groups(live, step)
    smallest[...] = jnp.ones((1, TILE), F32)

    def finish(tile, _):
        summed = jnp.sum(sums[:, at_tile(tile)], axis=0, keepdims=True)
        present = covered[tile] > 0
        value = highest + EPSILON * jnp.log(jnp.maximum(summed, TRUSTED))
        write_line(out_ref, tile, jnp.where(present, value, LOWEST))
        smallest[...] = jnp.minimum(smallest[...], jnp.where(present, summed, 1.0))
        return 0

    lax.fori_loop(0, target_tiles, finish, 0, unroll=UNROLL)

    @pl.when(jnp.min(smallest[...]) < TRUSTED)
    def _():
        for hbm, ref in ((source_hbm, source_ref), (target_hbm, target_ref)):
            copy = pltpu.make_async_copy(hbm, ref, semaphore)
            copy.start()
            copy.wait()
        general_lse(
            0, 1, list_ref, live,
            lambda tile: source_ref[:, at_tile(tile)].astype(F32),
            lambda tile: target_ref[:, at_tile(tile)].astype(F32),
            lambda tile: read_line(potential_ref, tile),
            out_ref, top, total,
        )


def row_call(own_list, counts, source_full, target_full, potential):
    source_cells, target_cells = source_full.shape[1], target_full.shape[1]
    slots = own_list.shape[1] // STORES
    return pl.pallas_call(
        row_kernel,
        name="row_sums",
        out_shape=(
            jax.ShapeDtypeStruct((source_cells // 128, 128), F32),
            pltpu.HBM(source_full.shape, BF16),
            pltpu.HBM(target_full.shape, BF16),
        )
        + (pltpu.VMEM((slots, TILE, TILE), BF16),) * STORES,
        in_specs=[HBM, SMEM, VMEM, VMEM, HBM],
        out_specs=(VMEM, HBM, HBM) + (VMEM,) * STORES,
        scratch_shapes=[
            pltpu.VMEM((source_cells, LEFT), BF16),
            pltpu.VMEM((RIGHT, target_cells), BF16),
            pltpu.VMEM((1, target_cells), F32),
            pltpu.VMEM((source_cells, 128), F32),
            pltpu.SMEM((source_cells // TILE,), jnp.int32),
            pltpu.VMEM((1, TILE), F32),
            pltpu.VMEM((8, source_cells), F32),
            pltpu.VMEM((8, source_cells), F32),
            pltpu.SMEM(own_list.shape, jnp.int32),
            pltpu.VMEM((target_cells // 128, 128), F32),
            pltpu.SemaphoreType.DMA((4,)),
        ],
        compiler_params=pltpu.CompilerParams(vmem_limit_bytes=14 << 20),
    )(in_hbm(own_list), counts, source_full, target_full, in_hbm(potential))


def column_call(own_list, counts, row_potential, stores, source_full, target_full):
    source_cells, target_cells = source_full.shape[1], target_full.shape[1]
    return pl.pallas_call(
        column_kernel,
        name="column_sums",
        out_shape=jax.ShapeDtypeStruct((target_cells // 128, 128), F32),
        in_specs=[HBM, SMEM, VMEM] + [VMEM] * STORES + [HBM, HBM],
        out_specs=VMEM,
        scratch_shapes=[
            pltpu.VMEM((16, source_cells), BF16),
            pltpu.VMEM((16, target_cells), F32),
            pltpu.SMEM((target_cells // TILE,), jnp.int32),
            pltpu.VMEM((1, TILE), F32),
            pltpu.VMEM((8, target_cells), F32),
            pltpu.VMEM((8, target_cells), F32),
            pltpu.VMEM((WIDTH, source_cells), BF16),
            pltpu.VMEM((WIDTH, target_cells), BF16),
            pltpu.SMEM(own_list.shape, jnp.int32),
            pltpu.SemaphoreType.DMA,
        ],
        compiler_params=pltpu.CompilerParams(vmem_limit_bytes=10 << 20),
    )(in_hbm(own_list), counts, row_potential, *stores, in_hbm(source_full), in_hbm(target_full))


def merged(parts):
    highest = functools.reduce(jnp.maximum, parts)
    summed = sum(jnp.exp((part - highest) * (1.0 / EPSILON)) for part in parts)
    return highest + EPSILON * jnp.log(summed)


def along(axis, size, group, stride, shift):
    pairs = []
    for index in range(size):
        digit = index // stride % group
        pairs.append((index, index + ((digit + shift) % group - digit) * stride))
    return lambda value: lax.ppermute(value, axis, pairs)


def local(source_embed, target_embed, target_potential, log_source_mass, log_target_mass, tile_list, counts):
    over_x = [along("src", 16, 4, 4, shift) for shift in (1, 2, 3)]
    over_z = [along("src", 16, 4, 1, shift) for shift in (1, 2, 3)]
    over_y = [along("tgt", 8, 4, 2, shift) for shift in (1, 2, 3)]
    over_core = along("tgt", 8, 2, 1, 1)

    sources = lax.axis_size("src")
    copies = pl.pallas_call(
        copies_kernel,
        name="target_copies",
        out_shape=pltpu.VMEM((sources,) + target_embed.shape, BF16),
        in_specs=[VMEM],
        out_specs=VMEM,
        compiler_params=pltpu.CompilerParams(vmem_limit_bytes=8 << 20),
    )(target_embed)
    target_full = lax.all_to_all(copies, "src", 0, 0).reshape(WIDTH, -1)
    source_full = lax.all_gather(source_embed, "tgt", axis=0, tiled=True)

    own_list = tile_list[0, 0]

    row, source_kept, target_kept, *stores = row_call(own_list, counts, source_full, target_full, target_potential.reshape(-1, 128))
    row = merged([row, over_core(row)])
    row = merged([row] + [send(row) for send in over_y])
    row_potential = EPSILON * log_source_mass.reshape(-1, 128) - row

    column = column_call(own_list, counts, row_potential, stores, source_kept, target_kept)
    column = merged([column] + [send(column) for send in over_x])
    column = merged([column] + [send(column) for send in over_z])
    column_potential = EPSILON * log_target_mass.reshape(-1, 128) - column
    return row_potential.reshape(-1), column_potential.reshape(-1)


def solution(mesh):
    return jax.shard_map(
        local,
        mesh=mesh,
        in_specs=(
            P("tgt", "src"),
            P("src", "tgt"),
            P("tgt"),
            P("src"),
            P("tgt"),
            P("src", "tgt", None, None),
            P("src", "tgt"),
        ),
        out_specs=(P("src"), P("tgt")),
        check_vma=False,
    )
```

```python
import functools

import jax
import jax.numpy as jnp
from jax import lax
from jax.experimental import pallas as pl
from jax.experimental.pallas import tpu as pltpu
from jax.sharding import PartitionSpec as P

TILE = 512
LINES = TILE // 128
WIDTH = 32
PIECES = 3
LEFT = 128
RIGHT = 112
DEPTH = 48
TOGETHER = 32
UNROLL = 8
STORES = 4
EPSILON = 0.1
KAPPA = 1.4426950408889634 / EPSILON
ALPHA = KAPPA / WIDTH
GAMMA = KAPPA / (2 * WIDTH)
LOWEST = -1e30
ABSENT = -1.0
TRUSTED = 2.0**-90

BF16, F32 = jnp.bfloat16, jnp.float32
VMEM = pl.BlockSpec(memory_space=pltpu.VMEM)
SMEM = pl.BlockSpec(memory_space=pltpu.SMEM)
HBM = pl.BlockSpec(memory_space=pltpu.HBM)


def in_hbm(value):
    return pltpu.with_memory_space_constraint(value, pltpu.HBM)


def at_tile(tile):
    return pl.ds(pl.multiple_of(tile * TILE, TILE), TILE)


def write_line(ref, tile, line):
    for part in range(LINES):
        ref[pl.ds(tile * LINES + part, 1), :] = line[:, part * 128 : (part + 1) * 128]


def read_line(ref, tile):
    return jnp.concatenate([ref[pl.ds(tile * LINES + part, 1), :] for part in range(LINES)], axis=1)


def highest_of(ref):
    return jnp.max(jnp.max(ref[...], axis=0, keepdims=True), axis=1, keepdims=True)


def pieces(value, number=PIECES):
    terms = []
    for _ in range(number):
        terms.append(value.astype(BF16).astype(F32))
        value = value - terms[-1]
    return terms


def squares(cells):
    return jnp.sum(cells * cells, axis=0, keepdims=True)


def general_lse(red_row, keep_row, list_ref, live, read_red, read_keep, read_bias, out_ref, top, total):
    keep_tiles = top.shape[1] // TILE
    half, scale = float(WIDTH), ALPHA
    rows_of = 64

    def clear(tile, _):
        at = at_tile(tile)
        top[:, at] = jnp.full((8, TILE), LOWEST, F32)
        total[:, at] = jnp.zeros((8, TILE), F32)
        return 0

    def step(entry, _):
        red_tile, keep_tile = list_ref[red_row, entry], list_ref[keep_row, entry]
        keep_at = at_tile(keep_tile)
        cells = read_red(red_tile)
        terms = pieces(half * read_bias(red_tile) - 0.5 * squares(cells))
        filler = jnp.zeros((DEPTH - WIDTH - PIECES, TILE), F32)
        left = jnp.transpose(jnp.concatenate([cells] + terms + [filler, jnp.zeros((LEFT - DEPTH, TILE), F32)], axis=0))
        left = left.astype(BF16)[:, :DEPTH]
        right = jnp.concatenate([read_keep(keep_tile), jnp.ones((PIECES, TILE), F32), filler], axis=0).astype(BF16)
        highest, summed = top[:, keep_at], total[:, keep_at]
        for row in range(0, TILE, rows_of):
            z = jnp.dot(left[row : row + rows_of], right, preferred_element_type=F32)
            z = z.reshape(rows_of // 8, 8, TILE) * scale
            higher = jnp.maximum(highest, jnp.max(z, axis=0))
            summed = summed * jnp.exp2(highest - higher) + jnp.sum(jnp.exp2(z - higher[None]), axis=0)
            highest = higher
        top[:, keep_at] = highest
        total[:, keep_at] = summed
        return 0

    def finish(tile, _):
        at = at_tile(tile)
        highest = jnp.max(top[:, at], axis=0, keepdims=True)
        summed = jnp.sum(total[:, at] * jnp.exp2(top[:, at] - highest), axis=0, keepdims=True)
        value = highest * (1.0 / KAPPA) + EPSILON * jnp.log(jnp.maximum(summed, 1.0))
        write_line(out_ref, tile, value - squares(read_keep(tile)) * (0.5 / WIDTH))
        return 0

    lax.fori_loop(0, keep_tiles, clear, 0)
    lax.fori_loop(0, live, step, 0)
    lax.fori_loop(0, keep_tiles, finish, 0)


def copies_kernel(part_ref, copies_ref):
    for copy in range(copies_ref.shape[0]):
        copies_ref[copy] = part_ref[...]


def source_rows(cells):
    rows = pieces(cells * ALPHA) + [jnp.ones((PIECES, TILE), F32)] + pieces(squares(cells) * -GAMMA)
    rows.append(jnp.zeros((LEFT - PIECES * WIDTH - 2 * PIECES, TILE), F32))
    return jnp.transpose(jnp.concatenate(rows, axis=0)).astype(BF16)


def groups(live, body):
    def one(group, _):
        for member in range(TOGETHER):
            entry = group * TOGETHER + member
            body(entry, member % STORES, entry // STORES)
        return 0

    lax.fori_loop(0, (live + TOGETHER - 1) // TOGETHER, one, 0)


def to_potentials(ref, highest):
    summed = ref[...]
    present = summed >= 0
    value = highest + EPSILON * jnp.log(jnp.maximum(summed, TRUSTED))
    ref[...] = jnp.where(present, value, LOWEST)
    return jnp.min(jnp.where(present, summed, 1.0))


def clear_marks(marks):
    for tile in range(marks.shape[0]):
        marks[tile] = 0


def row_kernel(
    list_hbm, count_ref, source_ref, target_ref, potential_hbm,
    out_ref, source_hbm, target_hbm, store_0, store_1, store_2, store_3,
    left_ref, right, weight, sums, covered, top, total, list_ref, potential_ref, semaphores,
):
    stores = (store_0, store_1, store_2, store_3)
    source_tiles = left_ref.shape[0] // TILE
    target_tiles = right.shape[1] // TILE
    live = count_ref[0, 0]
    rows_of = 64
    fetched = [
        pltpu.make_async_copy(potential_hbm, potential_ref, semaphores.at[2]),
        pltpu.make_async_copy(list_hbm, list_ref, semaphores.at[3]),
    ]
    for copy in fetched:
        copy.start()
    kept = [
        pltpu.make_async_copy(source_ref, source_hbm, semaphores.at[0]),
        pltpu.make_async_copy(target_ref, target_hbm, semaphores.at[1]),
    ]
    for copy in kept:
        copy.start()

    def prepare_source(tile, _):
        at = at_tile(tile)
        left_ref[at, :] = source_rows(source_ref[:, at].astype(F32))
        return 0

    clear_marks(covered)
    lax.fori_loop(0, source_tiles, prepare_source, 0, unroll=UNROLL)
    for copy in fetched:
        copy.wait()
    highest = highest_of(potential_ref)
    weight[...] = jnp.exp2((potential_ref[...] - highest) * KAPPA)

    def prepare(tile, _):
        at = at_tile(tile)
        cells = target_ref[:, at]
        for piece in range(PIECES):
            right[piece * WIDTH : (piece + 1) * WIDTH, at] = cells
        tail = pieces(squares(cells.astype(F32)) * -GAMMA) + [jnp.ones((PIECES, TILE), F32)]
        tail.append(jnp.zeros((RIGHT - PIECES * WIDTH - 2 * PIECES, TILE), F32))
        right[PIECES * WIDTH : RIGHT, at] = jnp.concatenate(tail, axis=0).astype(BF16)
        share = sums.shape[0] // target_tiles
        sums[pl.ds(pl.multiple_of(tile * share, share), share), :] = jnp.zeros((share, 128), F32)
        return 0

    lax.fori_loop(0, target_tiles, prepare, 0, unroll=UNROLL)

    def step(entry, store, slot):
        alive = (entry < live).astype(jnp.int32)
        source_tile = list_ref[0, entry]
        target_tile = list_ref[1, entry]
        covered[source_tile] = jnp.maximum(covered[source_tile], alive)
        factor = read_line(weight, target_tile) * alive.astype(F32)
        columns = right[:, at_tile(target_tile)]
        for row in range(0, TILE, rows_of):
            at = pl.ds(pl.multiple_of(source_tile * TILE + row, rows_of), rows_of)
            value = jnp.exp2(jnp.dot(left_ref[at, :RIGHT], columns, preferred_element_type=F32))
            stores[store][slot, row : row + rows_of, :] = value.astype(BF16)
            value = value * factor
            sums[at, :] += (value[:, 0:128] + value[:, 128:256]) + (value[:, 256:384] + value[:, 384:512])

    groups(live, step)
    def finish(tile, _):
        terms = jnp.concatenate(pieces(sums[at_tile(tile), :], 2), axis=1).astype(BF16)
        lines = lax.dot_general(jnp.ones((16, 256), BF16), terms, (((1,), (1,)), ((), ())), preferred_element_type=F32)
        write_line(out_ref, tile, jnp.where(covered[tile] > 0, jnp.maximum(lines[0:1], 0.0), ABSENT))
        return 0

    lax.fori_loop(0, source_tiles, finish, 0, unroll=UNROLL)
    smallest = to_potentials(out_ref, highest)
    for copy in kept:
        copy.wait()

    @pl.when(smallest < TRUSTED)
    def _():
        general_lse(
            1, 0, list_ref, live,
            lambda tile: target_ref[:, at_tile(tile)].astype(F32),
            lambda tile: source_ref[:, at_tile(tile)].astype(F32),
            lambda tile: read_line(potential_ref, tile),
            out_ref, top, total,
        )


def column_kernel(
    list_hbm, count_ref, potential_ref, store_0, store_1, store_2, store_3, source_hbm, target_hbm,
    out_ref,
    parts, weight, sums, covered, top, total, source_ref, target_ref, list_ref, semaphore,
):
    stores = (store_0, store_1, store_2, store_3)
    source_tiles = source_ref.shape[1] // TILE
    target_tiles = sums.shape[1] // TILE
    live = count_ref[0, 0]
    fetch = pltpu.make_async_copy(list_hbm, list_ref, semaphore)
    fetch.start()
    highest = highest_of(potential_ref)

    for piece, term in enumerate(pieces(jnp.exp2((potential_ref[...] - highest) * KAPPA))):
        parts[piece] = term

    def prepare(tile, _):
        terms = [read_line(parts.at[piece], tile) for piece in range(PIECES)]
        weight[:, at_tile(tile)] = jnp.concatenate(terms + [jnp.zeros((16 - PIECES, TILE), F32)], axis=0).astype(BF16)
        return 0

    def clear(tile, _):
        sums[:, at_tile(tile)] = jnp.zeros((16, TILE), F32)
        return 0

    clear_marks(covered)
    lax.fori_loop(0, source_tiles, prepare, 0, unroll=UNROLL)
    lax.fori_loop(0, target_tiles, clear, 0, unroll=UNROLL)
    fetch.wait()

    def step(entry, store, slot):
        alive = (entry < live).astype(jnp.int32)
        target_tile = list_ref[1, entry]
        covered[target_tile] = jnp.maximum(covered[target_tile], alive)
        lines = jnp.dot(weight[:, at_tile(list_ref[0, entry])], stores[store][slot], preferred_element_type=F32)
        sums[:, at_tile(target_tile)] += lines * alive.astype(F32)

    groups(live, step)
    def finish(tile, _):
        summed = jnp.sum(sums[:, at_tile(tile)], axis=0, keepdims=True)
        write_line(out_ref, tile, jnp.where(covered[tile] > 0, jnp.maximum(summed, 0.0), ABSENT))
        return 0

    lax.fori_loop(0, target_tiles, finish, 0, unroll=UNROLL)
    smallest = to_potentials(out_ref, highest)

    @pl.when(smallest < TRUSTED)
    def _():
        for hbm, ref in ((source_hbm, source_ref), (target_hbm, target_ref)):
            copy = pltpu.make_async_copy(hbm, ref, semaphore)
            copy.start()
            copy.wait()
        general_lse(
            0, 1, list_ref, live,
            lambda tile: source_ref[:, at_tile(tile)].astype(F32),
            lambda tile: target_ref[:, at_tile(tile)].astype(F32),
            lambda tile: read_line(potential_ref, tile),
            out_ref, top, total,
        )


def row_call(own_list, counts, source_full, target_full, potential):
    source_cells, target_cells = source_full.shape[1], target_full.shape[1]
    slots = own_list.shape[1] // STORES
    return pl.pallas_call(
        row_kernel,
        name="row_sums",
        out_shape=(
            jax.ShapeDtypeStruct((source_cells // 128, 128), F32),
            pltpu.HBM(source_full.shape, BF16),
            pltpu.HBM(target_full.shape, BF16),
        )
        + (pltpu.VMEM((slots, TILE, TILE), BF16),) * STORES,
        in_specs=[HBM, SMEM, VMEM, VMEM, HBM],
        out_specs=(VMEM, HBM, HBM) + (VMEM,) * STORES,
        scratch_shapes=[
            pltpu.VMEM((source_cells, LEFT), BF16),
            pltpu.VMEM((RIGHT, target_cells), BF16),
            pltpu.VMEM((target_cells // 128, 128), F32),
            pltpu.VMEM((source_cells, 128), F32),
            pltpu.SMEM((source_cells // TILE,), jnp.int32),
            pltpu.VMEM((8, source_cells), F32),
            pltpu.VMEM((8, source_cells), F32),
            pltpu.SMEM(own_list.shape, jnp.int32),
            pltpu.VMEM((target_cells // 128, 128), F32),
            pltpu.SemaphoreType.DMA((4,)),
        ],
        compiler_params=pltpu.CompilerParams(vmem_limit_bytes=14 << 20),
    )(in_hbm(own_list), counts, source_full, target_full, in_hbm(potential))


def column_call(own_list, counts, row_potential, stores, source_full, target_full):
    source_cells, target_cells = source_full.shape[1], target_full.shape[1]
    return pl.pallas_call(
        column_kernel,
        name="column_sums",
        out_shape=jax.ShapeDtypeStruct((target_cells // 128, 128), F32),
        in_specs=[HBM, SMEM, VMEM] + [VMEM] * STORES + [HBM, HBM],
        out_specs=VMEM,
        scratch_shapes=[
            pltpu.VMEM((PIECES, source_cells // 128, 128), F32),
            pltpu.VMEM((16, source_cells), BF16),
            pltpu.VMEM((16, target_cells), F32),
            pltpu.SMEM((target_cells // TILE,), jnp.int32),
            pltpu.VMEM((8, target_cells), F32),
            pltpu.VMEM((8, target_cells), F32),
            pltpu.VMEM((WIDTH, source_cells), BF16),
            pltpu.VMEM((WIDTH, target_cells), BF16),
            pltpu.SMEM(own_list.shape, jnp.int32),
            pltpu.SemaphoreType.DMA,
        ],
        compiler_params=pltpu.CompilerParams(vmem_limit_bytes=10 << 20),
    )(in_hbm(own_list), counts, row_potential, *stores, in_hbm(source_full), in_hbm(target_full))


def merged(parts):
    highest = functools.reduce(jnp.maximum, parts)
    summed = sum(jnp.exp((part - highest) * (1.0 / EPSILON)) for part in parts)
    return highest + EPSILON * jnp.log(summed)


def along(axis, size, group, stride, shift):
    pairs = []
    for index in range(size):
        digit = index // stride % group
        pairs.append((index, index + ((digit + shift) % group - digit) * stride))
    return lambda value: lax.ppermute(value, axis, pairs)


def local(source_embed, target_embed, target_potential, log_source_mass, log_target_mass, tile_list, counts):
    over_x = [along("src", 16, 4, 4, shift) for shift in (1, 2, 3)]
    over_z = [along("src", 16, 4, 1, shift) for shift in (1, 2, 3)]
    over_y = [along("tgt", 8, 4, 2, shift) for shift in (1, 2, 3)]
    over_core = along("tgt", 8, 2, 1, 1)

    sources = lax.axis_size("src")
    copies = pl.pallas_call(
        copies_kernel,
        name="target_copies",
        out_shape=pltpu.VMEM((sources,) + target_embed.shape, BF16),
        in_specs=[VMEM],
        out_specs=VMEM,
        compiler_params=pltpu.CompilerParams(vmem_limit_bytes=8 << 20),
    )(target_embed)
    target_full = lax.all_to_all(copies, "src", 0, 0).reshape(WIDTH, -1)
    source_full = lax.all_gather(source_embed, "tgt", axis=0, tiled=True)

    own_list = tile_list[0, 0]

    row, source_kept, target_kept, *stores = row_call(own_list, counts, source_full, target_full, target_potential.reshape(-1, 128))
    row = merged([row, over_core(row)])
    row = merged([row] + [send(row) for send in over_y])
    row_potential = EPSILON * log_source_mass.reshape(-1, 128) - row

    column = column_call(own_list, counts, row_potential, stores, source_kept, target_kept)
    column = merged([column] + [send(column) for send in over_x])
    column = merged([column] + [send(column) for send in over_z])
    column_potential = EPSILON * log_target_mass.reshape(-1, 128) - column
    return row_potential.reshape(-1), column_potential.reshape(-1)


def solution(mesh):
    return jax.shard_map(
        local,
        mesh=mesh,
        in_specs=(
            P("tgt", "src"),
            P("src", "tgt"),
            P("tgt"),
            P("src"),
            P("tgt"),
            P("src", "tgt", None, None),
            P("src", "tgt"),
        ),
        out_specs=(P("src"), P("tgt")),
        check_vma=False,
    )
```

```python
import functools

import jax
import jax.numpy as jnp
from jax import lax
from jax.experimental import pallas as pl
from jax.experimental.pallas import tpu as pltpu
from jax.sharding import PartitionSpec as P

TILE = 512
LINES = TILE // 128
WIDTH = 32
PIECES = 3
LEFT = 128
RIGHT = 112
DEPTH = 48
TOGETHER = 16
UNROLL = 8
STORES = 4
EPSILON = 0.1
KAPPA = 1.4426950408889634 / EPSILON
ALPHA = KAPPA / WIDTH
GAMMA = KAPPA / (2 * WIDTH)
LOWEST = -1e30
ABSENT = -1.0
TRUSTED = 2.0**-90

BF16, F32 = jnp.bfloat16, jnp.float32
VMEM = pl.BlockSpec(memory_space=pltpu.VMEM)
SMEM = pl.BlockSpec(memory_space=pltpu.SMEM)
HBM = pl.BlockSpec(memory_space=pltpu.HBM)


def in_hbm(value):
    return pltpu.with_memory_space_constraint(value, pltpu.HBM)


def at_tile(tile):
    return pl.ds(pl.multiple_of(tile * TILE, TILE), TILE)


def write_line(ref, tile, line):
    for part in range(LINES):
        ref[pl.ds(tile * LINES + part, 1), :] = line[:, part * 128 : (part + 1) * 128]


def read_line(ref, tile):
    return jnp.concatenate([ref[pl.ds(tile * LINES + part, 1), :] for part in range(LINES)], axis=1)


def highest_of(ref):
    return jnp.max(jnp.max(ref[...], axis=0, keepdims=True), axis=1, keepdims=True)


def pieces(value, number=PIECES):
    terms = []
    for _ in range(number):
        terms.append(value.astype(BF16).astype(F32))
        value = value - terms[-1]
    return terms


def squares(cells):
    return jnp.sum(cells * cells, axis=0, keepdims=True)


def general_lse(red_row, keep_row, list_ref, live, read_red, read_keep, read_bias, out_ref, top, total):
    keep_tiles = top.shape[1] // TILE
    half, scale = float(WIDTH), ALPHA
    rows_of = 64

    def clear(tile, _):
        at = at_tile(tile)
        top[:, at] = jnp.full((8, TILE), LOWEST, F32)
        total[:, at] = jnp.zeros((8, TILE), F32)
        return 0

    def step(entry, _):
        red_tile, keep_tile = list_ref[red_row, entry], list_ref[keep_row, entry]
        keep_at = at_tile(keep_tile)
        cells = read_red(red_tile)
        terms = pieces(half * read_bias(red_tile) - 0.5 * squares(cells))
        filler = jnp.zeros((DEPTH - WIDTH - PIECES, TILE), F32)
        left = jnp.transpose(jnp.concatenate([cells] + terms + [filler, jnp.zeros((LEFT - DEPTH, TILE), F32)], axis=0))
        left = left.astype(BF16)[:, :DEPTH]
        right = jnp.concatenate([read_keep(keep_tile), jnp.ones((PIECES, TILE), F32), filler], axis=0).astype(BF16)
        highest, summed = top[:, keep_at], total[:, keep_at]
        for row in range(0, TILE, rows_of):
            z = jnp.dot(left[row : row + rows_of], right, preferred_element_type=F32)
            z = z.reshape(rows_of // 8, 8, TILE) * scale
            higher = jnp.maximum(highest, jnp.max(z, axis=0))
            summed = summed * jnp.exp2(highest - higher) + jnp.sum(jnp.exp2(z - higher[None]), axis=0)
            highest = higher
        top[:, keep_at] = highest
        total[:, keep_at] = summed
        return 0

    def finish(tile, _):
        at = at_tile(tile)
        highest = jnp.max(top[:, at], axis=0, keepdims=True)
        summed = jnp.sum(total[:, at] * jnp.exp2(top[:, at] - highest), axis=0, keepdims=True)
        value = highest * (1.0 / KAPPA) + EPSILON * jnp.log(jnp.maximum(summed, 1.0))
        write_line(out_ref, tile, value - squares(read_keep(tile)) * (0.5 / WIDTH))
        return 0

    lax.fori_loop(0, keep_tiles, clear, 0)
    lax.fori_loop(0, live, step, 0)
    lax.fori_loop(0, keep_tiles, finish, 0)


def copies_kernel(part_ref, copies_ref):
    for copy in range(copies_ref.shape[0]):
        copies_ref[copy] = part_ref[...]


def source_rows(cells):
    rows = pieces(cells * ALPHA) + [jnp.ones((PIECES, TILE), F32)] + pieces(squares(cells) * -GAMMA)
    rows.append(jnp.zeros((LEFT - PIECES * WIDTH - 2 * PIECES, TILE), F32))
    return jnp.transpose(jnp.concatenate(rows, axis=0)).astype(BF16)


def groups(live, body):
    def one(group, _):
        for member in range(TOGETHER):
            entry = group * TOGETHER + member
            body(entry, member % STORES, entry // STORES)
        return 0

    lax.fori_loop(0, (live + TOGETHER - 1) // TOGETHER, one, 0)


def to_potentials(ref, highest):
    summed = ref[...]
    present = summed >= 0
    value = highest + EPSILON * jnp.log(jnp.maximum(summed, TRUSTED))
    ref[...] = jnp.where(present, value, LOWEST)
    return jnp.min(jnp.where(present, summed, 1.0))


def clear_marks(marks):
    for tile in range(marks.shape[0]):
        marks[tile] = 0


def row_kernel(
    list_hbm, count_ref, source_ref, target_ref, potential_hbm,
    out_ref, source_hbm, target_hbm, store_0, store_1, store_2, store_3,
    left_ref, right, weight, sums, covered, top, total, list_ref, potential_ref, semaphores,
):
    stores = (store_0, store_1, store_2, store_3)
    source_tiles = left_ref.shape[0] // TILE
    target_tiles = right.shape[1] // TILE
    live = count_ref[0, 0]
    rows_of = 64
    fetched = [
        pltpu.make_async_copy(potential_hbm, potential_ref, semaphores.at[2]),
        pltpu.make_async_copy(list_hbm, list_ref, semaphores.at[3]),
    ]
    for copy in fetched:
        copy.start()
    kept = [
        pltpu.make_async_copy(source_ref, source_hbm, semaphores.at[0]),
        pltpu.make_async_copy(target_ref, target_hbm, semaphores.at[1]),
    ]
    for copy in kept:
        copy.start()

    def prepare_source(tile, _):
        at = at_tile(tile)
        left_ref[at, :] = source_rows(source_ref[:, at].astype(F32))
        return 0

    clear_marks(covered)
    lax.fori_loop(0, source_tiles, prepare_source, 0, unroll=UNROLL)
    for copy in fetched:
        copy.wait()
    highest = highest_of(potential_ref)
    weight[...] = jnp.exp2((potential_ref[...] - highest) * KAPPA)

    def prepare(tile, _):
        at = at_tile(tile)
        cells = target_ref[:, at]
        for piece in range(PIECES):
            right[piece * WIDTH : (piece + 1) * WIDTH, at] = cells
        tail = pieces(squares(cells.astype(F32)) * -GAMMA) + [jnp.ones((PIECES, TILE), F32)]
        tail.append(jnp.zeros((RIGHT - PIECES * WIDTH - 2 * PIECES, TILE), F32))
        right[PIECES * WIDTH : RIGHT, at] = jnp.concatenate(tail, axis=0).astype(BF16)
        share = sums.shape[0] // target_tiles
        sums[pl.ds(pl.multiple_of(tile * share, share), share), :] = jnp.zeros((share, 128), F32)
        return 0

    lax.fori_loop(0, target_tiles, prepare, 0, unroll=UNROLL)

    def step(entry, store, slot):
        alive = (entry < live).astype(jnp.int32)
        source_tile = list_ref[0, entry]
        target_tile = list_ref[1, entry]
        covered[source_tile] = jnp.maximum(covered[source_tile], alive)
        factor = read_line(weight, target_tile) * alive.astype(F32)
        columns = right[:, at_tile(target_tile)]
        for row in range(0, TILE, rows_of):
            at = pl.ds(pl.multiple_of(source_tile * TILE + row, rows_of), rows_of)
            value = jnp.exp2(jnp.dot(left_ref[at, :RIGHT], columns, preferred_element_type=F32))
            stores[store][slot, row : row + rows_of, :] = value.astype(BF16)
            value = value * factor
            sums[at, :] += (value[:, 0:128] + value[:, 128:256]) + (value[:, 256:384] + value[:, 384:512])

    groups(live, step)
    def finish(tile, _):
        terms = jnp.concatenate(pieces(sums[at_tile(tile), :], 2), axis=1).astype(BF16)
        lines = lax.dot_general(jnp.ones((16, 256), BF16), terms, (((1,), (1,)), ((), ())), preferred_element_type=F32)
        write_line(out_ref, tile, jnp.where(covered[tile] > 0, jnp.maximum(lines[0:1], 0.0), ABSENT))
        return 0

    lax.fori_loop(0, source_tiles, finish, 0, unroll=UNROLL)
    smallest = to_potentials(out_ref, highest)
    for copy in kept:
        copy.wait()

    @pl.when(smallest < TRUSTED)
    def _():
        general_lse(
            1, 0, list_ref, live,
            lambda tile: target_ref[:, at_tile(tile)].astype(F32),
            lambda tile: source_ref[:, at_tile(tile)].astype(F32),
            lambda tile: read_line(potential_ref, tile),
            out_ref, top, total,
        )


def column_kernel(
    list_hbm, count_ref, potential_ref, store_0, store_1, store_2, store_3, source_hbm, target_hbm,
    out_ref,
    parts, weight, sums, covered, top, total, source_ref, target_ref, list_ref, semaphore,
):
    stores = (store_0, store_1, store_2, store_3)
    source_tiles = source_ref.shape[1] // TILE
    target_tiles = sums.shape[1] // TILE
    live = count_ref[0, 0]
    fetch = pltpu.make_async_copy(list_hbm, list_ref, semaphore)
    fetch.start()
    highest = highest_of(potential_ref)

    for piece, term in enumerate(pieces(jnp.exp2((potential_ref[...] - highest) * KAPPA))):
        parts[piece] = term

    def prepare(tile, _):
        terms = [read_line(parts.at[piece], tile) for piece in range(PIECES)]
        weight[:, at_tile(tile)] = jnp.concatenate(terms + [jnp.zeros((16 - PIECES, TILE), F32)], axis=0).astype(BF16)
        return 0

    def clear(tile, _):
        sums[:, at_tile(tile)] = jnp.zeros((16, TILE), F32)
        return 0

    clear_marks(covered)
    lax.fori_loop(0, source_tiles, prepare, 0, unroll=UNROLL)
    lax.fori_loop(0, target_tiles, clear, 0, unroll=UNROLL)
    fetch.wait()

    def step(entry, store, slot):
        alive = (entry < live).astype(jnp.int32)
        target_tile = list_ref[1, entry]
        covered[target_tile] = jnp.maximum(covered[target_tile], alive)
        lines = jnp.dot(weight[:, at_tile(list_ref[0, entry])], stores[store][slot], preferred_element_type=F32)
        sums[:, at_tile(target_tile)] += lines * alive.astype(F32)

    groups(live, step)
    def finish(tile, _):
        summed = jnp.sum(sums[:, at_tile(tile)], axis=0, keepdims=True)
        write_line(out_ref, tile, jnp.where(covered[tile] > 0, jnp.maximum(summed, 0.0), ABSENT))
        return 0

    lax.fori_loop(0, target_tiles, finish, 0, unroll=UNROLL)
    smallest = to_potentials(out_ref, highest)

    @pl.when(smallest < TRUSTED)
    def _():
        for hbm, ref in ((source_hbm, source_ref), (target_hbm, target_ref)):
            copy = pltpu.make_async_copy(hbm, ref, semaphore)
            copy.start()
            copy.wait()
        general_lse(
            0, 1, list_ref, live,
            lambda tile: source_ref[:, at_tile(tile)].astype(F32),
            lambda tile: target_ref[:, at_tile(tile)].astype(F32),
            lambda tile: read_line(potential_ref, tile),
            out_ref, top, total,
        )


def row_call(own_list, counts, source_full, target_full, potential):
    source_cells, target_cells = source_full.shape[1], target_full.shape[1]
    slots = own_list.shape[1] // STORES
    return pl.pallas_call(
        row_kernel,
        name="row_sums",
        out_shape=(
            jax.ShapeDtypeStruct((source_cells // 128, 128), F32),
            pltpu.HBM(source_full.shape, BF16),
            pltpu.HBM(target_full.shape, BF16),
        )
        + (pltpu.VMEM((slots, TILE, TILE), BF16),) * STORES,
        in_specs=[HBM, SMEM, VMEM, VMEM, HBM],
        out_specs=(VMEM, HBM, HBM) + (VMEM,) * STORES,
        scratch_shapes=[
            pltpu.VMEM((source_cells, LEFT), BF16),
            pltpu.VMEM((RIGHT, target_cells), BF16),
            pltpu.VMEM((target_cells // 128, 128), F32),
            pltpu.VMEM((source_cells, 128), F32),
            pltpu.SMEM((source_cells // TILE,), jnp.int32),
            pltpu.VMEM((8, source_cells), F32),
            pltpu.VMEM((8, source_cells), F32),
            pltpu.SMEM(own_list.shape, jnp.int32),
            pltpu.VMEM((target_cells // 128, 128), F32),
            pltpu.SemaphoreType.DMA((4,)),
        ],
        compiler_params=pltpu.CompilerParams(vmem_limit_bytes=14 << 20),
    )(in_hbm(own_list), counts, source_full, target_full, in_hbm(potential))


def column_call(own_list, counts, row_potential, stores, source_full, target_full):
    source_cells, target_cells = source_full.shape[1], target_full.shape[1]
    return pl.pallas_call(
        column_kernel,
        name="column_sums",
        out_shape=jax.ShapeDtypeStruct((target_cells // 128, 128), F32),
        in_specs=[HBM, SMEM, VMEM] + [VMEM] * STORES + [HBM, HBM],
        out_specs=VMEM,
        scratch_shapes=[
            pltpu.VMEM((PIECES, source_cells // 128, 128), F32),
            pltpu.VMEM((16, source_cells), BF16),
            pltpu.VMEM((16, target_cells), F32),
            pltpu.SMEM((target_cells // TILE,), jnp.int32),
            pltpu.VMEM((8, target_cells), F32),
            pltpu.VMEM((8, target_cells), F32),
            pltpu.VMEM((WIDTH, source_cells), BF16),
            pltpu.VMEM((WIDTH, target_cells), BF16),
            pltpu.SMEM(own_list.shape, jnp.int32),
            pltpu.SemaphoreType.DMA,
        ],
        compiler_params=pltpu.CompilerParams(vmem_limit_bytes=10 << 20),
    )(in_hbm(own_list), counts, row_potential, *stores, in_hbm(source_full), in_hbm(target_full))


def merged(parts):
    highest = functools.reduce(jnp.maximum, parts)
    summed = sum(jnp.exp((part - highest) * (1.0 / EPSILON)) for part in parts)
    return highest + EPSILON * jnp.log(summed)


def along(axis, size, group, stride, shift):
    pairs = []
    for index in range(size):
        digit = index // stride % group
        pairs.append((index, index + ((digit + shift) % group - digit) * stride))
    return lambda value: lax.ppermute(value, axis, pairs)


def local(source_embed, target_embed, target_potential, log_source_mass, log_target_mass, tile_list, counts):
    over_x = [along("src", 16, 4, 4, shift) for shift in (1, 2, 3)]
    over_z = [along("src", 16, 4, 1, shift) for shift in (1, 2, 3)]
    over_y = [along("tgt", 8, 4, 2, shift) for shift in (1, 2, 3)]
    over_core = along("tgt", 8, 2, 1, 1)

    sources = lax.axis_size("src")
    copies = pl.pallas_call(
        copies_kernel,
        name="target_copies",
        out_shape=pltpu.VMEM((sources,) + target_embed.shape, BF16),
        in_specs=[VMEM],
        out_specs=VMEM,
        compiler_params=pltpu.CompilerParams(vmem_limit_bytes=8 << 20),
    )(target_embed)
    target_full = lax.all_to_all(copies, "src", 0, 0).reshape(WIDTH, -1)
    source_full = lax.all_gather(source_embed, "tgt", axis=0, tiled=True)

    own_list = tile_list[0, 0]

    row, source_kept, target_kept, *stores = row_call(own_list, counts, source_full, target_full, target_potential.reshape(-1, 128))
    row = merged([row, over_core(row)])
    row = merged([row] + [send(row) for send in over_y])
    row_potential = EPSILON * log_source_mass.reshape(-1, 128) - row

    column = column_call(own_list, counts, row_potential, stores, source_kept, target_kept)
    column = merged([column] + [send(column) for send in over_x])
    column = merged([column] + [send(column) for send in over_z])
    column_potential = EPSILON * log_target_mass.reshape(-1, 128) - column
    return row_potential.reshape(-1), column_potential.reshape(-1)


def solution(mesh):
    return jax.shard_map(
        local,
        mesh=mesh,
        in_specs=(
            P("tgt", "src"),
            P("src", "tgt"),
            P("tgt"),
            P("src"),
            P("tgt"),
            P("src", "tgt", None, None),
            P("src", "tgt"),
        ),
        out_specs=(P("src"), P("tgt")),
        check_vma=False,
    )
```
